256 devices in a mesh: fsdp: 16 (over z, core), expert: 16 (over y, x).
Axes of the slice: x: 4, y: 4, z: 8, core: 2. Of those that a mesh axis runs over, the one named last changes fastest.
Arguments:
- tokens: bfloat16 [32768, 4096], P(('fsdp', 'expert')), may hold values from -6 to 6
- cotangent: bfloat16 [32768, 4096], P(('fsdp', 'expert')), may hold values from -24 to 24
- routed_expert_index: int32 [32768, 2], P(('fsdp', 'expert')), may hold values from 0 to 15, all different within a row; in each aligned block of 128 rows (0 to 127, 128 to 255, ...) at most 20 rows name the same one
- router_gate_weights: bfloat16 [32768, 2], P(('fsdp', 'expert')), may hold values from 0.049804688 to 1
- token_tenant_index: int32 [32768], P(('fsdp', 'expert')), may hold values from 0 to 3
- frozen_gate_weight: bfloat16 [16, 4096, 768], P('expert', 'fsdp'), may hold values from -0.09375 to 0.09375
- frozen_up_weight: bfloat16 [16, 4096, 768], P('expert', 'fsdp'), may hold values from -0.09375 to 0.09375
- frozen_down_weight: bfloat16 [16, 768, 4096], P('expert', None, 'fsdp'), may hold values from -0.21875 to 0.21875
- adapter_first_factors: bfloat16 [16, 768, 128], P('expert', 'fsdp'), may hold values from -0.21875 to 0.21875
- adapter_second_factors: bfloat16 [16, 128, 4096], P('expert', None, 'fsdp'), may hold values from -1 to 1
Outputs:
- token_input_gradient: bfloat16 [32768, 4096], P(('fsdp', 'expert'))
- gate_weight_gradient: bfloat16 [32768, 2], P(('fsdp', 'expert'))
- adapter_first_gradient: float32 [16, 768, 128], P('expert', 'fsdp')
- adapter_second_gradient: float32 [16, 128, 4096], P('expert', None, 'fsdp')
The draws below stay inside these ranges and needn't reach their ends.
Inputs may be any that keep to these rules, and one draw needn't show every extreme that they name: `routed_expert_index`: within each aligned block of 128 tokens (the tokens of one device) no expert is named more than 20 times, a bound that some block reaches; the 2 experts of a token differ.
All inputs are finite; a program needn't handle non-finite values.
Results may differ from the reference program's by a relative error of at most 0.0069.
Values may be sent and summed in bfloat16 or wider, within the bound.
No kernel may reach another device: no remote copies, remote signals or barrier semaphores. Data moves between devices by JAX's collectives and lax.ppermute only.
A program may use at most 128 MiB of HBM per device.

```python
import math
import jax
import jax.numpy as jnp
import numpy as np
from jax import lax

MODEL_WIDTH = 4096
HIDDEN_HALF = 768
ADAPTER_RANK = 32
TENANT_COUNT = 4
TOP = 2
TOK_DEV = 128
WINDOW_EXPERTS = 16
CAP = 20
TOKENS = 32768
N_FSDP = 16
N_EXPERT = 16


def touch_ends(values, stream_key, smallest, top_value):
    longest = values.shape.index(max(values.shape))
    spots = []
    for shift in (0, 1):
        where = [jax.random.randint(jax.random.fold_in(stream_key, axis), (), 0, length) for axis, length in enumerate(values.shape)]
        where[longest] = (where[longest] + shift) % values.shape[longest]
        spots.append(tuple(where))
    return values.at[spots[0]].set(smallest).at[spots[1]].set(top_value)


def raised(values, own_key, source, target, parts, factor):
    owner, partner = [(jnp.arange(values.shape[position]) // (values.shape[position] // parts)).reshape([-1 if axis == position else 1 for axis in range(values.ndim)]) for position in (source, target)]
    chosen = jax.random.permutation(own_key, parts)[partner]
    strong = (owner == chosen) | (owner == (partner + parts // 2) % parts)
    return jnp.where(strong, factor * values, values)


def shard_levels(stream_key, shape, cuts, smallest, largest):
    factor_of = 1.0
    for axis_at, shards_of in cuts:
        heights = jax.random.uniform(jax.random.fold_in(jax.random.fold_in(stream_key, 6), axis_at), (shards_of,), jnp.float32, smallest / len(cuts), largest / len(cuts))
        factor_of = factor_of * jnp.repeat(jnp.exp(heights), shape[axis_at] // shards_of).reshape((-1,) + (1,) * (len(shape) - 1 - axis_at))
    return factor_of


def assign_block(stream_key, own, number, rows, number_of, top, reach, slope):
    order = jax.random.permutation(stream_key, number_of)
    heavy_load, ordinary = portions_of(number_of, rows * top, reach, slope, True), portions_of(number_of, rows * top, reach, slope, False)
    places = jnp.arange(number_of)

    def named(tallies, turn):
        used = int((tallies > 0).sum())
        fixed = max(1, used // 4)
        moved = fixed + (places - fixed + turn * (used - fixed)) % max(1, number_of - fixed)
        return jnp.zeros((number_of,), jnp.int32).at[order[jnp.where(places < fixed, places, moved)]].set(jnp.asarray(tallies, jnp.int32))

    tallies = jnp.where(number % 4 == 0, named(heavy_load, number // 4), named(ordinary, number - number // 4 - 1))
    mixed = jax.random.permutation(jax.random.fold_in(own, 3), number_of)
    giver, taker = mixed[0:number_of // 2 * 2:2], mixed[1:number_of // 2 * 2:2]
    room = jnp.minimum(tallies[giver] - 1, reach - tallies[taker]) // 2
    room = jnp.where((giver == order[0]) | (taker == order[0]) | (tallies[taker] == 0), 0, jnp.maximum(room, 0))
    moved = jax.random.randint(jax.random.fold_in(own, 4), (number_of // 2,), 0, 1 << 20) % (room + 1)
    tallies = tallies.at[giver].add(-moved).at[taker].add(moved)
    items = jnp.searchsorted(jnp.cumsum(tallies), jnp.arange(rows * top), side="right").astype(jnp.int32)
    grid = items.reshape(top, rows).T
    grid = grid[jax.random.permutation(jax.random.fold_in(own, 1), rows)]
    turn = jax.random.randint(jax.random.fold_in(own, 2), (rows, 1), 0, top)
    return jnp.take_along_axis(grid, (jnp.arange(top)[None, :] + turn) % top, axis=1)


def portions_of(amount, total, limit, slope, full):
    loads = [(1 << 20) // math.isqrt(standing ** slope) + 1 for standing in range(1, amount + 1)]
    largest = limit if full else min(limit, max(-(-total // amount), total * loads[0] // sum(loads)))
    least = 1 if total - largest >= amount - 1 else 0
    given, spare = [largest] + [least] * (amount - 1), total - largest - least * (amount - 1)
    while spare > 0:
        candidates = [i for i in range(1, amount) if given[i] < largest] or [i for i in range(1, amount) if given[i] < limit]
        mass, budget = sum([loads[i] for i in candidates]), spare
        for i in candidates:
            extra = min(limit - given[i], max(1, budget * loads[i] // mass), spare)
            given[i] = given[i] + extra
            spare = spare - extra
    return np.array(given)


def scatter_about(key, shape, deviation, reach, pieces=(), kind=jnp.bfloat16):
    drawn = deviation * jax.random.normal(key, shape, jnp.float32)
    if pieces:
        drawn = drawn * shard_levels(key, shape, pieces, -0.22, 0.18)
    return jnp.clip(drawn, -reach, reach).astype(kind)


def bell_draw_with(own_key, shape, deviation, most, shards, heavy, kind=jnp.bfloat16):
    array = deviation * jax.random.normal(own_key, shape, jnp.float32)
    if shards:
        array = array * shard_levels(own_key, shape, shards, -0.22, 0.18)
    return jnp.clip(raised(array, jax.random.fold_in(own_key, 3), *heavy), -most, most).astype(kind)


def setup_inputs(seed: int = 0) -> dict:
    arg_keys = jax.random.split(jax.random.key(seed), 11)
    tokens = scatter_about(arg_keys[0], (TOKENS, MODEL_WIDTH), 1.0, 6.0, ((0, 256),))
    cotangent = bell_draw_with(arg_keys[1], (TOKENS, MODEL_WIDTH), 1.0, 24.0, ((0, 256),), (0, 1, 256, 6.0))
    routed_expert_index_keys = jax.random.split(jax.random.fold_in(arg_keys[2], 1), TOKENS // TOK_DEV)
    routed_expert_index_turns = jax.random.permutation(jax.random.fold_in(arg_keys[2], 3), TOKENS // TOK_DEV)
    routed_expert_index = jax.vmap(lambda own, number: assign_block(jax.random.fold_in(arg_keys[2], 2), own, number, TOK_DEV, WINDOW_EXPERTS, TOP, CAP, 1))(routed_expert_index_keys, routed_expert_index_turns).reshape((TOKENS, TOP))
    router_gate_weights = jnp.clip(jnp.exp(math.log(1.0) - 2.9996462 * jax.random.uniform(arg_keys[3], (TOKENS, TOP), jnp.float32) ** shard_levels(arg_keys[3], (TOKENS, TOP), ((0, 256),), -0.2, 0.2)), 0.049804688, 1.0).astype(jnp.bfloat16)
    token_tenant_index = touch_ends(jax.random.randint(arg_keys[4], (TOKENS,), 0, TENANT_COUNT), jax.random.fold_in(arg_keys[4], 1), 0, TENANT_COUNT - 1).astype(jnp.int32)
    frozen_gate_weight = scatter_about(arg_keys[5], (WINDOW_EXPERTS, MODEL_WIDTH, HIDDEN_HALF), MODEL_WIDTH ** -0.5, 0.09375, ((0, 16), (1, 16)))
    frozen_up_weight = scatter_about(arg_keys[6], (WINDOW_EXPERTS, MODEL_WIDTH, HIDDEN_HALF), MODEL_WIDTH ** -0.5, 0.09375, ((0, 16), (1, 16)))
    frozen_down_weight = scatter_about(arg_keys[7], (WINDOW_EXPERTS, HIDDEN_HALF, MODEL_WIDTH), HIDDEN_HALF ** -0.5, 0.21875, ((0, 16), (2, 16)))
    adapter_first_factors = scatter_about(arg_keys[8], (WINDOW_EXPERTS, HIDDEN_HALF, TENANT_COUNT * ADAPTER_RANK), HIDDEN_HALF ** -0.5, 0.21875, ((0, 16), (1, 16)))
    adapter_second_factors = scatter_about(arg_keys[9], (WINDOW_EXPERTS, TENANT_COUNT * ADAPTER_RANK, MODEL_WIDTH), ADAPTER_RANK ** -0.5, 1.0, ((0, 16), (2, 16)))
    return dict(tokens=tokens, cotangent=cotangent, routed_expert_index=routed_expert_index, router_gate_weights=router_gate_weights, token_tenant_index=token_tenant_index, frozen_gate_weight=frozen_gate_weight, frozen_up_weight=frozen_up_weight, frozen_down_weight=frozen_down_weight, adapter_first_factors=adapter_first_factors, adapter_second_factors=adapter_second_factors)


adapter_scale = 2.0


def contract_matrices(left_side, right_side, left_dim, right_dim):
    return lax.dot_general(left_side, right_side, (((left_dim,), (right_dim,)), ((), ())), preferred_element_type=jnp.float32)


def finish_backward(routed_token_rows, cotangent_rows, gate_value_rows, tenant_column_mask, gate_preactivation, up_preactivation, frozen_gate_weight, frozen_up_weight, frozen_down_weight, adapter_first_factors, adapter_second_factors):
    sigmoid_gate = jax.nn.sigmoid(gate_preactivation)
    activated = gate_preactivation * sigmoid_gate
    hidden_units = (activated * up_preactivation).astype(jnp.bfloat16)
    adapter_rank_mask = jnp.repeat(tenant_column_mask, ADAPTER_RANK, axis=1)
    reduced_product = (contract_matrices(hidden_units, adapter_first_factors, 1, 0) * adapter_rank_mask).astype(jnp.bfloat16)
    expert_output = contract_matrices(hidden_units, frozen_down_weight, 1, 0) + adapter_scale * contract_matrices(reduced_product, adapter_second_factors, 1, 0)
    gate_dot = jnp.sum(cotangent_rows.astype(jnp.float32) * expert_output, axis=1).astype(jnp.bfloat16)
    scaled_cotangent = (gate_value_rows.astype(jnp.float32)[:, None] * cotangent_rows.astype(jnp.float32)).astype(jnp.bfloat16)
    reduced_gradient = (adapter_scale * contract_matrices(scaled_cotangent, adapter_second_factors, 1, 1) * adapter_rank_mask).astype(jnp.bfloat16)
    hidden_gradient = contract_matrices(scaled_cotangent, frozen_down_weight, 1, 1) + contract_matrices(reduced_gradient, adapter_first_factors, 1, 1)
    gate_part = (hidden_gradient * up_preactivation * sigmoid_gate * (1.0 + gate_preactivation * (1.0 - sigmoid_gate))).astype(jnp.bfloat16)
    up_part = (hidden_gradient * activated).astype(jnp.bfloat16)
    row_grad = (contract_matrices(gate_part, frozen_gate_weight, 1, 1) + contract_matrices(up_part, frozen_up_weight, 1, 1)).astype(jnp.bfloat16)
    first_factor_gradient = contract_matrices(hidden_units, reduced_gradient, 0, 0)
    second_factor_gradient = adapter_scale * contract_matrices(reduced_product, scaled_cotangent, 0, 0)
    return row_grad, gate_dot, first_factor_gradient, second_factor_gradient


def reference(tokens, cotangent, routed_expert_index, router_gate_weights, token_tenant_index, frozen_gate_weight, frozen_up_weight, frozen_down_weight, adapter_first_factors, adapter_second_factors):
    blocks = N_FSDP * N_EXPERT
    block_ids = routed_expert_index.reshape(blocks, TOK_DEV * TOP)
    onehot = (block_ids[:, :, None] == jnp.arange(WINDOW_EXPERTS, dtype=jnp.int32)[None, None, :]).astype(jnp.int32)
    before = jnp.cumsum(onehot, axis=1) - onehot
    slot_index = jnp.sum(before * onehot, axis=2)
    block_base = jnp.arange(blocks, dtype=jnp.int32)[:, None] * CAP
    column = (block_base + slot_index).reshape(-1).astype(jnp.int32)
    flat_ids = routed_expert_index.reshape(-1).astype(jnp.int32)
    assign = jnp.arange(TOKENS * TOP, dtype=jnp.int32)
    slot_count = blocks * CAP
    source_token_index = jnp.zeros((WINDOW_EXPERTS, slot_count), jnp.int32).at[flat_ids, column].set(assign)
    filled_rows = jnp.zeros((WINDOW_EXPERTS, slot_count), jnp.bfloat16).at[flat_ids, column].set(1.0)
    gate_flat = router_gate_weights.reshape(-1)
    tenant_range = jnp.arange(TENANT_COUNT, dtype=jnp.int32)

    def single_expert_pass(running, per_expert):
        input_gradient_sums, gate_gradient_sums = running
        source_row, filled_row, gate_w, up_w, down_w, adapter_a, adapter_b = per_expert
        token_of = source_row // TOP
        routed_token_rows = tokens[token_of] * filled_row[:, None]
        cotangent_rows = cotangent[token_of] * filled_row[:, None]
        gate_value_rows = gate_flat[source_row] * filled_row
        tenant_column_mask = (token_tenant_index[token_of][:, None] == tenant_range[None, :]).astype(jnp.bfloat16) * filled_row[:, None]
        gate_preactivation = contract_matrices(routed_token_rows, gate_w, 1, 0)
        up_preactivation = contract_matrices(routed_token_rows, up_w, 1, 0)
        row_grad, gate_dot, first_factor_gradient, second_factor_gradient = finish_backward(routed_token_rows, cotangent_rows, gate_value_rows, tenant_column_mask, gate_preactivation, up_preactivation, gate_w, up_w, down_w, adapter_a, adapter_b)
        input_gradient_sums = input_gradient_sums.at[token_of].add(row_grad.astype(jnp.float32))
        gate_gradient_sums = gate_gradient_sums.at[source_row].add(gate_dot.astype(jnp.float32))
        return (input_gradient_sums, gate_gradient_sums), (first_factor_gradient, second_factor_gradient)

    start_offset = (jnp.zeros((TOKENS, MODEL_WIDTH), jnp.float32), jnp.zeros((TOKENS * TOP,), jnp.float32))
    (input_gradient_sums, gate_gradient_sums), (first_factor_gradient, second_factor_gradient) = lax.scan(single_expert_pass, start_offset, (source_token_index, filled_rows, frozen_gate_weight, frozen_up_weight, frozen_down_weight, adapter_first_factors, adapter_second_factors))
    return input_gradient_sums.astype(jnp.bfloat16), gate_gradient_sums.reshape(TOKENS, TOP).astype(jnp.bfloat16), first_factor_gradient, second_factor_gradient
```

```python
import jax
import jax.numpy as jnp
from jax import lax
from jax.experimental import pallas as pl
from jax.experimental.pallas import tpu as pltpu
from jax.sharding import PartitionSpec as P

RANK = 32
TENANTS = 4
ADAPTER_SCALE = 2.0
CAPACITY = 20
MAIN = 16
SPARE = CAPACITY - MAIN
QUARTERS = MAIN // SPARE
LANES = 128
SPARE_LANE = 8
TILE = 256

bf16 = jnp.bfloat16
f32 = jnp.float32


def contract(left, right, left_dim, right_dim):
    return lax.dot_general(
        left, right, (((left_dim,), (right_dim,)), ((), ())), preferred_element_type=f32
    )


def iota(shape, dim):
    return lax.broadcasted_iota(jnp.int32, shape, dim)


def slot_places(ids, experts):
    rows, top = ids.shape
    lower = (iota((rows, rows), 1) < iota((rows, rows), 0)).astype(f32).astype(bf16)
    named = iota((rows, LANES), 1)
    total = jnp.zeros((1, LANES), f32)
    places = []
    for j in range(top):
        expert = ids[:, j : j + 1]
        onehot = (named == expert).astype(f32)
        before = contract(lower, onehot.astype(bf16), 1, 0) + total
        total = total + jnp.sum(onehot, axis=0, keepdims=True)
        rank = jnp.sum(before * onehot, axis=1, keepdims=True).astype(jnp.int32)
        main = jnp.where(rank < MAIN, expert * MAIN + rank, -1)
        spare = jnp.where(rank < MAIN, -MAIN * experts, expert * MAIN + rank - MAIN)
        places.append((main, spare))
    return places


def placed(place, slots):
    return (iota((place.shape[0], slots), 1) == place).astype(f32).astype(bf16)


def dispatch_kernel(ids_ref, gate_ref, tenant_ref, tok_ref, cot_ref, x_ref, c_ref, experts):
    width = tok_ref.shape[1]
    part = width // QUARTERS
    slots = experts * MAIN
    places = slot_places(ids_ref[...], experts)
    main = sum(placed(m, slots) for m, _ in places)
    spare = [sum(placed(s + SPARE * q, slots) for _, s in places) for q in range(QUARTERS)]
    for src, dst in ((tok_ref, x_ref), (cot_ref, c_ref)):
        for q in range(QUARTERS):
            cols = slice(q * part, (q + 1) * part)
            dst[:, cols] = contract(main, src[:, cols], 0, 0).astype(bf16)
        last = jnp.zeros((slots, part), f32)
        for q in range(QUARTERS):
            last = last + contract(spare[q], src[:, q * part : (q + 1) * part], 0, 0)
        dst[:, width : width + part] = last.astype(bf16)
    lane = iota((tok_ref.shape[0], LANES), 1)
    tenant = tenant_ref[...]
    meta = jnp.zeros((slots, LANES), f32)
    for j, (m, s) in enumerate(places):
        gate = gate_ref[:, j : j + 1].astype(f32)
        for place, base in ((m, 0), (s, SPARE_LANE)):
            cols = jnp.where(lane == base, gate, (lane - base - 1 == tenant).astype(f32))
            meta = meta + contract(placed(place, slots), cols.astype(bf16), 0, 0)
    c_ref[:, width + part :] = meta.astype(bf16)


def combine_kernel(ids_ref, r_ref, tok_ref, gate_ref, experts):
    width = tok_ref.shape[1]
    part = width // QUARTERS
    slots = experts * MAIN
    places = slot_places(ids_ref[...], experts)
    main = sum(placed(m, slots) for m, _ in places)
    for q in range(QUARTERS):
        spare = sum(placed(s + SPARE * q, slots) for _, s in places)
        cols = slice(q * part, (q + 1) * part)
        both = contract(main, r_ref[:, cols], 1, 0) + contract(
            spare, r_ref[:, width : width + part], 1, 0
        )
        tok_ref[:, cols] = both.astype(bf16)
    meta = r_ref[:, width + part :]
    for j, (m, s) in enumerate(places):
        a = contract(placed(m, slots), meta, 1, 0)[:, 0:1]
        b = contract(placed(s, slots), meta, 1, 0)[:, SPARE_LANE : SPARE_LANE + 1]
        gate_ref[:, j : j + 1] = (a + b).astype(bf16)


def expert_kernel(
    where_ref, x_hbm, c_hbm, w_hbm, a1_ref,
    rg_ref, own_ref, other_ref,
    xs, cs, xo, co, meta_ref, w, acc, hid, hga, parts, spare_rows, first, lowt, sems,
):
    width = w.shape[0]
    half = hid.shape[1]
    rank_all = a1_ref.shape[1]
    part = width // QUARTERS
    slots = x_hbm.shape[0]
    spares = slots // QUARTERS
    rows = slots + spares
    wide = 2 * half

    copies = {}

    def begin(name, src, dst):
        copies[name] = pltpu.make_async_copy(src, dst, sems.at[len(copies)])
        copies[name].start()

    begin("xo", x_hbm.at[:, pl.ds(width, part)], xo)
    begin("co", c_hbm.at[:, pl.ds(width, part)], co)
    for q in range(QUARTERS):
        cols = pl.ds(q * part, part)
        begin(("x", q), x_hbm.at[:, cols], xs.at[pl.ds(0, slots), cols])
        begin(("w", q), w_hbm.at[cols, :], w.at[cols, :])
        begin(("c", q), c_hbm.at[:, cols], cs.at[pl.ds(0, slots), cols])
    begin("meta", c_hbm.at[:, pl.ds(width + part, LANES)], meta_ref)

    def chosen(q):
        row = iota((spares, slots), 0)
        return (
            iota((spares, slots), 1) == (row >> 2) * MAIN + q * SPARE + (row & 3)
        ).astype(f32).astype(bf16)

    copies["xo"].wait()
    copies["co"].wait()
    for q in range(QUARTERS):
        cols = slice(q * part, (q + 1) * part)
        sel = chosen(q)
        xs[slots:, cols] = contract(sel, xo[...], 1, 0).astype(bf16)
        cs[slots:, cols] = contract(sel, co[...], 1, 0).astype(bf16)
    for q in range(QUARTERS):
        cols = slice(q * part, (q + 1) * part)

        def product(rows_ref, at, size):
            out = pl.ds(at, size)
            got = contract(rows_ref[:, cols], w[cols, out], 1, 0)
            if q == 0:
                acc[:, out] = got
            else:
                acc[:, out] += got

        copies[("x", q)].wait()
        copies[("w", q)].wait()

        @pl.loop(0, wide // TILE)
        def _(n):
            product(xs, pl.multiple_of(n * TILE, TILE), TILE)

        copies[("c", q)].wait()

        @pl.loop(0, half // TILE)
        def _(n):
            product(cs, pl.multiple_of(wide + n * TILE, TILE), TILE)

        product(cs, wide + half, rank_all)

    copies["meta"].wait()
    meta = meta_ref[...]
    meta_spare = contract(chosen(0), meta, 1, 0).astype(bf16)
    lane_in, lane_out = iota((LANES, rank_all), 0), iota((LANES, rank_all), 1)

    def spread(base):
        mask = (lane_in - base - 1 == lane_out // RANK).astype(f32).astype(bf16)
        gate = (lane_in == base).astype(f32).astype(bf16)
        return mask, gate

    mask_0, gate_0 = spread(0)
    mask_s, gate_s = spread(SPARE_LANE)
    mask = jnp.concatenate(
        [contract(meta, mask_0, 1, 0), contract(meta_spare, mask_s, 1, 0)], axis=0
    )
    gate = jnp.concatenate(
        [contract(meta, gate_0, 1, 0), contract(meta_spare, gate_s, 1, 0)], axis=0
    )

    step = 32

    @pl.loop(0, rows // step)
    def _(i):
        r = pl.ds(pl.multiple_of(i * step, step), step)
        pre_gate, pre_up = acc[r, :half], acc[r, half:wide]
        hid[r, :] = (pre_gate * jax.nn.sigmoid(pre_gate) * pre_up).astype(bf16)

    a1 = a1_ref[...]
    cot_low = acc[:, wide + half :] * mask
    low = (contract(hid[...], a1, 1, 0) * mask).astype(bf16)
    low_grad = (ADAPTER_SCALE * gate * cot_low).astype(bf16)
    hga[...] = contract(low_grad, a1, 1, 1)
    acc[:, wide + half :] = ADAPTER_SCALE * low.astype(f32) * cot_low
    lowt[...] = (ADAPTER_SCALE * gate * low.astype(f32)).astype(bf16)
    first[...] = contract(hid[...], low_grad, 0, 0)
    xs[:, :LANES] = gate.astype(bf16)

    @pl.loop(0, rows // step)
    def _(i):
        r = pl.ds(pl.multiple_of(i * step, step), step)
        pre_gate, pre_up, cot_down = acc[r, :half], acc[r, half:wide], acc[r, wide : wide + half]
        s = jax.nn.sigmoid(pre_gate)
        grad = xs[r, 0:1].astype(f32) * cot_down + hga[r, :]
        parts[r, half:] = (grad * (pre_gate * s)).astype(bf16)
        parts[r, :half] = (grad * pre_up * s * (1.0 + pre_gate * (1.0 - s))).astype(bf16)
        dot = jnp.sum(hid[r, :].astype(f32) * cot_down, axis=1, keepdims=True) + jnp.sum(
            acc[r, wide + half :], axis=1, keepdims=True
        )
        xs[r, LANES : 2 * LANES] = jnp.broadcast_to(dot, (step, LANES)).astype(bf16)

    @pl.loop(0, width // TILE)
    def _(d):
        cols = pl.ds(pl.multiple_of(d * TILE, TILE), TILE)
        got = contract(parts[...], w[cols, :wide], 1, 1).astype(bf16)
        rg_ref[:, cols] = got[:slots]
        spare_rows[:, cols] = got[slots:]

    last = jnp.zeros((slots, part), f32)
    for q in range(QUARTERS):
        last = last + contract(chosen(q), spare_rows[:, q * part : (q + 1) * part], 0, 0)
    rg_ref[:, width : width + part] = last.astype(bf16)
    dots = xs[:, LANES : 2 * LANES].astype(f32)
    lane = iota((slots, LANES), 1)
    spare_dots = contract(chosen(0), dots[slots:].astype(bf16), 0, 0)
    rg_ref[:, width + part :] = jnp.where(
        lane == 0, dots[:slots], jnp.where(lane == SPARE_LANE, spare_dots, 0.0)
    ).astype(bf16)

    z, core = where_ref[0], where_ref[1]
    zs = own_ref.shape[0]
    share = first.shape[0] // (2 * zs)

    @pl.loop(0, zs)
    def _(dz):
        for ref, side in ((own_ref, core), (other_ref, 1 - core)):
            f = lax.rem(z + dz, zs) * 2 + side
            cols = pl.ds(pl.multiple_of(f * TILE, TILE), TILE)
            ref[dz, :rank_all, :] = contract(lowt[...], cs[:, cols], 0, 0).astype(bf16)
            at = pl.multiple_of(f * share, 16)
            block = first[pl.ds(at, share), :].astype(bf16)
            ref[dz, rank_all : rank_all + 16, :rank_all] = block[:16]
            ref[dz, rank_all : rank_all + 16, rank_all:] = block[16:32]
            ref[dz, rank_all + 16 :, :rank_all] = block[32:48]
            ref[dz, rank_all + 16 :, rank_all:] = jnp.zeros((16, TILE - rank_all), bf16)


VMEM = pl.BlockSpec(memory_space=pltpu.VMEM)
ANY = pl.BlockSpec(memory_space=pl.ANY)
SMEM = pl.BlockSpec(memory_space=pltpu.SMEM)


def shards(
    tokens,
    cotangent,
    routed_expert_index,
    router_gate_weights,
    token_tenant_index,
    frozen_gate_weight,
    frozen_up_weight,
    frozen_down_weight,
    adapter_first_factors,
    adapter_second_factors,
):
    experts, spread = lax.axis_size("expert"), lax.axis_size("fsdp")
    tok_rows, top = routed_expert_index.shape
    width = tokens.shape[1]
    half = frozen_gate_weight.shape[2]
    ranks = adapter_first_factors.shape[2]
    part = width // QUARTERS
    slots = experts * MAIN
    spares = slots // QUARTERS
    rows = slots + spares
    cols = 3 * half + ranks
    zs = spread // 2
    here = lax.axis_index("fsdp")
    where = jnp.stack([here // 2, here % 2]).astype(jnp.int32)

    packed = jnp.concatenate(
        [
            frozen_gate_weight[0],
            frozen_up_weight[0],
            frozen_down_weight[0].T,
            adapter_second_factors[0].T,
        ],
        axis=1,
    )
    weights = lax.all_gather(packed, "fsdp", axis=0, tiled=True)

    x_send, c_send = pl.pallas_call(
        lambda *refs: dispatch_kernel(*refs, experts=experts),
        out_shape=(
            jax.ShapeDtypeStruct((slots, width + part), bf16),
            jax.ShapeDtypeStruct((slots, width + part + LANES), bf16),
        ),
        in_specs=[VMEM] * 5,
        out_specs=(VMEM, VMEM),
        compiler_params=pltpu.CompilerParams(vmem_limit_bytes=40 << 20),
    )(
        routed_expert_index,
        router_gate_weights,
        token_tenant_index.reshape(tok_rows, 1),
        tokens,
        cotangent,
    )

    def exchange(rows_2d):
        block = rows_2d.reshape(experts, MAIN, rows_2d.shape[1])
        return lax.all_to_all(block, "expert", split_axis=0, concat_axis=0, tiled=True).reshape(
            rows_2d.shape
        )

    x_rows, c_rows = exchange(x_send), exchange(c_send)
    first_full = lax.all_to_all(
        jnp.broadcast_to(adapter_first_factors, (spread,) + adapter_first_factors.shape[1:]),
        "fsdp",
        split_axis=0,
        concat_axis=0,
        tiled=True,
    ).reshape(half, ranks)

    back, own, other = pl.pallas_call(
        expert_kernel,
        out_shape=(
            jax.ShapeDtypeStruct((slots, width + part + LANES), bf16),
            jax.ShapeDtypeStruct((zs, ranks + 32, TILE), bf16),
            jax.ShapeDtypeStruct((zs, ranks + 32, TILE), bf16),
        ),
        in_specs=[SMEM, ANY, ANY, ANY, VMEM],
        out_specs=(VMEM, VMEM, VMEM),
        scratch_shapes=[
            pltpu.VMEM((rows, width), bf16),
            pltpu.VMEM((rows, width), bf16),
            pltpu.VMEM((slots, part), bf16),
            pltpu.VMEM((slots, part), bf16),
            pltpu.VMEM((slots, LANES), bf16),
            pltpu.VMEM((width, cols), bf16),
            pltpu.VMEM((rows, cols), f32),
            pltpu.VMEM((rows, half), bf16),
            pltpu.VMEM((rows, half), f32),
            pltpu.VMEM((rows, 2 * half), bf16),
            pltpu.VMEM((spares, width), bf16),
            pltpu.VMEM((half, ranks), f32),
            pltpu.VMEM((rows, ranks), bf16),
            pltpu.SemaphoreType.DMA((3 + 3 * QUARTERS,)),
        ],
        compiler_params=pltpu.CompilerParams(vmem_limit_bytes=52 << 20),
    )(where, x_rows, c_rows, weights, first_full)

    returned = exchange(back)

    swap = [(f, f ^ 1) for f in range(spread)]
    pair = own.astype(f32) + lax.ppermute(other, "fsdp", swap).astype(f32)
    halved = pair.astype(bf16)
    total = pair[0]
    for dz in range(1, zs):
        moves = [(f, (f + 2 * dz) % spread) for f in range(spread)]
        total = total + lax.ppermute(halved[dz], "fsdp", moves).astype(f32)
    adapter_second_gradient = total[None, :ranks]
    adapter_first_gradient = jnp.concatenate(
        [
            total[ranks : ranks + 16, :ranks],
            total[ranks : ranks + 16, ranks:],
            total[ranks + 16 :, :ranks],
        ],
        axis=0,
    )[None]

    token_input_gradient, gate_weight_gradient = pl.pallas_call(
        lambda *refs: combine_kernel(*refs, experts=experts),
        out_shape=(
            jax.ShapeDtypeStruct((tok_rows, width), bf16),
            jax.ShapeDtypeStruct((tok_rows, top), bf16),
        ),
        in_specs=[VMEM] * 2,
        out_specs=(VMEM, VMEM),
        compiler_params=pltpu.CompilerParams(vmem_limit_bytes=32 << 20),
    )(routed_expert_index, returned)
    return (
        token_input_gradient,
        gate_weight_gradient,
        adapter_first_gradient,
        adapter_second_gradient,
    )


def solution(mesh):
    in_specs = (
        P(("fsdp", "expert"), None),
        P(("fsdp", "expert"), None),
        P(("fsdp", "expert"), None),
        P(("fsdp", "expert"), None),
        P(("fsdp", "expert")),
        P("expert", "fsdp", None),
        P("expert", "fsdp", None),
        P("expert", None, "fsdp"),
        P("expert", "fsdp", None),
        P("expert", None, "fsdp"),
    )
    out_specs = (
        P(("fsdp", "expert"), None),
        P(("fsdp", "expert"), None),
        P("expert", "fsdp", None),
        P("expert", None, "fsdp"),
    )
    return jax.shard_map(shards, mesh=mesh, in_specs=in_specs, out_specs=out_specs, check_vma=False)
```

```python
import jax
import jax.numpy as jnp
from jax import lax
from jax.experimental import pallas as pl
from jax.experimental.pallas import tpu as pltpu
from jax.sharding import PartitionSpec as P

RANK = 32
TENANTS = 4
ADAPTER_SCALE = 2.0
CAPACITY = 20
MAIN = 16
SPARE = CAPACITY - MAIN
QUARTERS = MAIN // SPARE
LANES = 128
SPARE_LANE = 8
TILE = 256
CHUNKS = 4
LIMIT = 54
BACK = 1024

bf16 = jnp.bfloat16
f32 = jnp.float32


def contract(left, right, left_dim, right_dim):
    return lax.dot_general(
        left, right, (((left_dim,), (right_dim,)), ((), ())), preferred_element_type=f32
    )


def iota(shape, dim):
    return lax.broadcasted_iota(jnp.int32, shape, dim)


def slot_places(ids, experts):
    rows, top = ids.shape
    lower = (iota((rows, rows), 1) < iota((rows, rows), 0)).astype(f32).astype(bf16)
    named = iota((rows, LANES), 1)
    total = jnp.zeros((1, LANES), f32)
    places = []
    for j in range(top):
        expert = ids[:, j : j + 1]
        onehot = (named == expert).astype(f32)
        before = contract(lower, onehot.astype(bf16), 1, 0) + total
        total = total + jnp.sum(onehot, axis=0, keepdims=True)
        rank = jnp.sum(before * onehot, axis=1, keepdims=True).astype(jnp.int32)
        main = jnp.where(rank < MAIN, expert * MAIN + rank, -1)
        spare = jnp.where(rank < MAIN, -MAIN * experts, expert * MAIN + rank - MAIN)
        places.append((main, spare))
    return places


def placed(place, slots):
    return (iota((place.shape[0], slots), 1) == place).astype(f32).astype(bf16)


def pack_kernel(gate_hbm, up_hbm, down_hbm, second_hbm, out_hbm, down, second, turned, sems):
    half = gate_hbm.shape[1]
    cols = out_hbm.shape[1]
    load_down = pltpu.make_async_copy(down_hbm, down, sems.at[0])
    load_second = pltpu.make_async_copy(second_hbm, second, sems.at[1])
    gate = pltpu.make_async_copy(gate_hbm, out_hbm.at[:, pl.ds(0, half)], sems.at[2])
    up = pltpu.make_async_copy(up_hbm, out_hbm.at[:, pl.ds(half, half)], sems.at[3])
    store = pltpu.make_async_copy(turned, out_hbm.at[:, pl.ds(2 * half, cols - 2 * half)], sems.at[4])
    for copy in (load_down, load_second, gate, up):
        copy.start()
    load_down.wait()
    turned[:, :half] = down[...].T
    load_second.wait()
    turned[:, half:] = second[...].T
    store.start()
    gate.wait()
    up.wait()
    store.wait()


def dispatch_kernel(ids_ref, gate_ref, tenant_ref, tok_ref, cot_ref, x_ref, c_ref, experts):
    width = tok_ref.shape[1]
    part = width // QUARTERS
    slots = experts * MAIN
    places = slot_places(ids_ref[...], experts)
    main = sum(placed(m, slots) for m, _ in places)
    spare = [sum(placed(s + SPARE * q, slots) for _, s in places) for q in range(QUARTERS)]
    for src, dst in ((tok_ref, x_ref), (cot_ref, c_ref)):
        for q in range(QUARTERS):
            cols = slice(q * part, (q + 1) * part)
            dst[:, cols] = contract(main, src[:, cols], 0, 0).astype(bf16)
        last = jnp.zeros((slots, part), f32)
        for q in range(QUARTERS):
            last = last + contract(spare[q], src[:, q * part : (q + 1) * part], 0, 0)
        dst[:, width : width + part] = last.astype(bf16)
    lane = iota((tok_ref.shape[0], LANES), 1)
    tenant = tenant_ref[...]
    meta = jnp.zeros((slots, LANES), f32)
    for j, (m, s) in enumerate(places):
        gate = gate_ref[:, j : j + 1].astype(f32)
        for place, base in ((m, 0), (s, SPARE_LANE)):
            cols = jnp.where(lane == base, gate, (lane - base - 1 == tenant).astype(f32))
            meta = meta + contract(placed(place, slots), cols.astype(bf16), 0, 0)
    c_ref[:, width + part :] = meta.astype(bf16)


def combine_kernel(ids_ref, r_ref, tok_ref, gate_ref, experts):
    width = tok_ref.shape[1]
    part = width // QUARTERS
    slots = experts * MAIN
    places = slot_places(ids_ref[...], experts)
    main = sum(placed(m, slots) for m, _ in places)
    for q in range(QUARTERS):
        spare = sum(placed(s + SPARE * q, slots) for _, s in places)
        cols = slice(q * part, (q + 1) * part)
        both = contract(main, r_ref[:, cols], 1, 0) + contract(
            spare, r_ref[:, width : width + part], 1, 0
        )
        tok_ref[:, cols] = both.astype(bf16)
    meta = r_ref[:, width + part :]
    for j, (m, s) in enumerate(places):
        a = contract(placed(m, slots), meta, 1, 0)[:, 0:1]
        b = contract(placed(s, slots), meta, 1, 0)[:, SPARE_LANE : SPARE_LANE + 1]
        gate_ref[:, j : j + 1] = (a + b).astype(bf16)


def chosen(q, spares, slots):
    row = iota((spares, slots), 0)
    return (
        (iota((spares, slots), 1) == (row >> 2) * MAIN + q * SPARE + (row & 3))
        .astype(f32)
        .astype(bf16)
    )


def unfold_rows(src_ref, dst_ref):
    width = dst_ref.shape[1]
    part = width // QUARTERS
    slots = src_ref.shape[0]
    spares = slots // QUARTERS
    dst_ref[:slots, :] = src_ref[:, :width]
    for q in range(QUARTERS):
        dst_ref[slots:, q * part : (q + 1) * part] = contract(
            chosen(q, spares, slots), src_ref[:, width : width + part], 1, 0
        ).astype(bf16)


def unfold_cot_kernel(src_ref, dst_ref, mask_ref, gate_ref):
    unfold_rows(src_ref, dst_ref)
    slots = src_ref.shape[0]
    spares = slots // QUARTERS
    lanes = mask_ref.shape[1]
    meta = src_ref[:, src_ref.shape[1] - LANES :]
    meta_spare = contract(chosen(0, spares, slots), meta, 1, 0).astype(bf16)
    lane_in, lane_out = iota((LANES, lanes), 0), iota((LANES, lanes), 1)
    for rows, block, base in ((slice(0, slots), meta, 0), (slice(slots, None), meta_spare, SPARE_LANE)):
        tenant = (lane_in - base - 1 == lane_out // RANK).astype(f32).astype(bf16)
        weight = (lane_in == base).astype(f32).astype(bf16)
        mask_ref[rows, :] = contract(block, tenant, 1, 0)
        gate_ref[rows, :] = contract(block, weight, 1, 0)


def expert_kernel(
    x_hbm, c_hbm, w_hbm, a1_hbm, mask_hbm, gate_hbm,
    rg_hbm, hid_hbm, low_grad_hbm, lowt_hbm,
    xs, cs, w, a1_ref, mask_ref, gate_ref,
    rg_ref, hid, low_grad_ref, lowt_ref,
    acc, hga, parts, spare_rows, dots, sems,
):
    rows, width = xs.shape
    half = hid.shape[1]
    part = width // QUARTERS
    slots = rg_ref.shape[0]
    spares = rows - slots
    wide = 2 * half
    depth = width // CHUNKS

    pending = []

    def begin(src, dst):
        copy = pltpu.make_async_copy(src, dst, sems.at[len(pending)])
        copy.start()
        pending.append(copy)
        return copy

    chunks = []
    for q in range(CHUNKS):
        cols = pl.ds(q * depth, depth)
        chunks.append(
            (
                begin(x_hbm.at[:, cols], xs.at[:, cols]),
                begin(w_hbm.at[cols, :], w.at[cols, :]),
                begin(c_hbm.at[:, cols], cs.at[:, cols]),
            )
        )
    small = [begin(a1_hbm, a1_ref), begin(mask_hbm, mask_ref), begin(gate_hbm, gate_ref)]

    for q in range(CHUNKS):
        cols = slice(q * depth, (q + 1) * depth)
        for copy in chunks[q]:
            copy.wait()
        for rows_ref, out in ((xs, slice(0, wide)), (cs, slice(wide, None))):
            got = contract(rows_ref[:, cols], w[cols, out], 1, 0)
            if q == 0:
                acc[:, out] = got
            else:
                acc[:, out] += got
    for copy in small:
        copy.wait()

    step = 320

    @pl.loop(0, rows // step)
    def _(i):
        r = pl.ds(pl.multiple_of(i * step, step), step)
        pre_gate, pre_up = acc[r, :half], acc[r, half:wide]
        hid[r, :] = (pre_gate * jax.nn.sigmoid(pre_gate) * pre_up).astype(bf16)

    mask, gate = mask_ref[...], gate_ref[...]
    a1 = a1_ref[...]
    cot_low = acc[:, wide + half :] * mask
    low_grad = (ADAPTER_SCALE * gate * cot_low).astype(bf16)
    low_grad_ref[...] = low_grad
    hga[...] = contract(low_grad, a1, 1, 1)
    low = (contract(hid[...], a1, 1, 0) * mask).astype(bf16).astype(f32)
    acc[:, wide + half :] = ADAPTER_SCALE * low * cot_low
    lowt_ref[...] = (ADAPTER_SCALE * gate * low).astype(bf16)

    @pl.loop(0, rows // step)
    def _(i):
        r = pl.ds(pl.multiple_of(i * step, step), step)
        pre_gate, pre_up, cot_down = acc[r, :half], acc[r, half:wide], acc[r, wide : wide + half]
        s = jax.nn.sigmoid(pre_gate)
        grad = gate_ref[r, 0:1] * cot_down + hga[r, :]
        parts[r, half:] = (grad * (pre_gate * s)).astype(bf16)
        parts[r, :half] = (grad * pre_up * s * (1.0 + pre_gate * (1.0 - s))).astype(bf16)
        dot = jnp.sum(hid[r, :].astype(f32) * cot_down, axis=1, keepdims=True) + jnp.sum(
            acc[r, wide + half :], axis=1, keepdims=True
        )
        dots[r, :] = jnp.broadcast_to(dot, (step, LANES)).astype(bf16)

    sent = [
        begin(hid, hid_hbm),
        begin(low_grad_ref, low_grad_hbm),
        begin(lowt_ref, lowt_hbm),
    ]
    lane = iota((slots, LANES), 1)
    spare_dots = contract(chosen(0, spares, slots), dots[slots:, :], 0, 0)
    rg_ref[:, width + part :] = jnp.where(
        lane == 0, dots[:slots, :].astype(f32), jnp.where(lane == SPARE_LANE, spare_dots, 0.0)
    ).astype(bf16)
    for d in range(width // BACK):
        cols = slice(d * BACK, (d + 1) * BACK)
        got = contract(parts[...], w[cols, :wide], 1, 1).astype(bf16)
        rg_ref[:, cols] = got[:slots]
        spare_rows[:, cols] = got[slots:]
        place = pl.ds(d * BACK, BACK)
        sent.append(begin(rg_ref.at[:, place], rg_hbm.at[:, place]))

    last = jnp.zeros((slots, part), f32)
    for q in range(QUARTERS):
        last = last + contract(
            chosen(q, spares, slots), spare_rows[:, q * part : (q + 1) * part], 0, 0
        )
    rg_ref[:, width : width + part] = last.astype(bf16)
    place = pl.ds(width, part + LANES)
    sent.append(begin(rg_ref.at[:, place], rg_hbm.at[:, place]))
    for copy in sent:
        copy.wait()


def adapter_kernel(where_ref, hid_ref, low_grad_ref, lowt_ref, c_ref, own_ref, other_ref, first):
    ranks = low_grad_ref.shape[1]
    z, core = where_ref[0], where_ref[1]
    zs = own_ref.shape[0]
    share = first.shape[0] // (2 * zs)
    first[...] = contract(hid_ref[...], low_grad_ref[...], 0, 0)
    lowt = lowt_ref[...].T

    @pl.loop(0, zs)
    def _(dz):
        for ref, side in ((other_ref, 1 - core), (own_ref, core)):
            f = lax.rem(z + dz, zs) * 2 + side
            cols = pl.ds(pl.multiple_of(f * TILE, TILE), TILE)
            ref[dz, :ranks, :] = contract(lowt, c_ref[:, cols], 1, 0).astype(bf16)
            at = pl.multiple_of(f * share, 16)
            block = first[pl.ds(at, share), :].astype(bf16)
            ref[dz, ranks : ranks + 16, :ranks] = block[:16]
            ref[dz, ranks : ranks + 16, ranks:] = block[16:32]
            ref[dz, ranks + 16 :, :ranks] = block[32:48]
            ref[dz, ranks + 16 :, ranks:] = jnp.zeros((16, TILE - ranks), bf16)


VMEM = pl.BlockSpec(memory_space=pltpu.VMEM)
ANY = pl.BlockSpec(memory_space=pl.ANY)
SMEM = pl.BlockSpec(memory_space=pltpu.SMEM)


def shards(
    tokens,
    cotangent,
    routed_expert_index,
    router_gate_weights,
    token_tenant_index,
    frozen_gate_weight,
    frozen_up_weight,
    frozen_down_weight,
    adapter_first_factors,
    adapter_second_factors,
):
    experts, spread = lax.axis_size("expert"), lax.axis_size("fsdp")
    tok_rows, top = routed_expert_index.shape
    width = tokens.shape[1]
    half = frozen_gate_weight.shape[2]
    ranks = adapter_first_factors.shape[2]
    part = width // QUARTERS
    slots = experts * MAIN
    spares = slots // QUARTERS
    rows = slots + spares
    cols = 3 * half + ranks
    shard = frozen_gate_weight.shape[1]
    zs = spread // 2
    here = lax.axis_index("fsdp")
    where = jnp.stack([here // 2, here % 2]).astype(jnp.int32)

    packed = pl.pallas_call(
        pack_kernel,
        name="pack_weights",
        out_shape=jax.ShapeDtypeStruct((shard, cols), bf16),
        in_specs=[ANY] * 4,
        out_specs=ANY,
        scratch_shapes=[
            pltpu.VMEM((half, shard), bf16),
            pltpu.VMEM((ranks, shard), bf16),
            pltpu.VMEM((shard, half + ranks), bf16),
            pltpu.SemaphoreType.DMA((5,)),
        ],
        compiler_params=pltpu.CompilerParams(vmem_limit_bytes=60 << 20),
    )(
        frozen_gate_weight[0],
        frozen_up_weight[0],
        frozen_down_weight[0],
        adapter_second_factors[0],
    )
    weights = lax.all_gather(packed, "fsdp", axis=0, tiled=True)

    x_send, c_send = pl.pallas_call(
        lambda *refs: dispatch_kernel(*refs, experts=experts),
        out_shape=(
            jax.ShapeDtypeStruct((slots, width + part), bf16),
            jax.ShapeDtypeStruct((slots, width + part + LANES), bf16),
        ),
        in_specs=[VMEM] * 5,
        out_specs=(VMEM, VMEM),
        compiler_params=pltpu.CompilerParams(vmem_limit_bytes=40 << 20),
    )(
        routed_expert_index,
        router_gate_weights,
        token_tenant_index.reshape(tok_rows, 1),
        tokens,
        cotangent,
    )

    def exchange(rows_2d):
        block = rows_2d.reshape(experts, MAIN, rows_2d.shape[1])
        return lax.all_to_all(block, "expert", split_axis=0, concat_axis=0, tiled=True).reshape(
            rows_2d.shape
        )

    x_rows, c_rows = exchange(x_send), exchange(c_send)
    first_full = lax.all_to_all(
        jnp.broadcast_to(adapter_first_factors, (spread,) + adapter_first_factors.shape[1:]),
        "fsdp",
        split_axis=0,
        concat_axis=0,
        tiled=True,
    ).reshape(half, ranks)

    x_all = pl.pallas_call(
        unfold_rows,
        name="unfold_tokens",
        out_shape=jax.ShapeDtypeStruct((rows, width), bf16),
        in_specs=[VMEM],
        out_specs=VMEM,
        compiler_params=pltpu.CompilerParams(vmem_limit_bytes=24 << 20),
    )(x_rows)
    c_all, mask, gate = pl.pallas_call(
        unfold_cot_kernel,
        name="unfold_cotangent",
        out_shape=(
            jax.ShapeDtypeStruct((rows, width), bf16),
            jax.ShapeDtypeStruct((rows, ranks), f32),
            jax.ShapeDtypeStruct((rows, ranks), f32),
        ),
        in_specs=[VMEM],
        out_specs=(VMEM, VMEM, VMEM),
        compiler_params=pltpu.CompilerParams(vmem_limit_bytes=24 << 20),
    )(c_rows)

    back, hidden, low_grad, low_rank = pl.pallas_call(
        expert_kernel,
        name="expert",
        out_shape=(
            jax.ShapeDtypeStruct((slots, width + part + LANES), bf16),
            jax.ShapeDtypeStruct((rows, half), bf16),
            jax.ShapeDtypeStruct((rows, ranks), bf16),
            jax.ShapeDtypeStruct((rows, ranks), bf16),
        ),
        in_specs=[ANY] * 6,
        out_specs=(ANY, ANY, ANY, ANY),
        scratch_shapes=[
            pltpu.VMEM((rows, width), bf16),
            pltpu.VMEM((rows, width), bf16),
            pltpu.VMEM((width, cols), bf16),
            pltpu.VMEM((half, ranks), bf16),
            pltpu.VMEM((rows, ranks), f32),
            pltpu.VMEM((rows, ranks), f32),
            pltpu.VMEM((slots, width + part + LANES), bf16),
            pltpu.VMEM((rows, half), bf16),
            pltpu.VMEM((rows, ranks), bf16),
            pltpu.VMEM((rows, ranks), bf16),
            pltpu.VMEM((rows, cols), f32),
            pltpu.VMEM((rows, half), f32),
            pltpu.VMEM((rows, 2 * half), bf16),
            pltpu.VMEM((spares, width), bf16),
            pltpu.VMEM((rows, LANES), bf16),
            pltpu.SemaphoreType.DMA((3 * CHUNKS + 7 + width // BACK,)),
        ],
        compiler_params=pltpu.CompilerParams(vmem_limit_bytes=LIMIT << 20),
    )(x_all, c_all, weights, first_full, mask, gate)

    own, other = pl.pallas_call(
        adapter_kernel,
        name="adapters",
        out_shape=(
            jax.ShapeDtypeStruct((zs, ranks + 32, TILE), bf16),
            jax.ShapeDtypeStruct((zs, ranks + 32, TILE), bf16),
        ),
        in_specs=[SMEM, VMEM, VMEM, VMEM, VMEM],
        out_specs=(VMEM, VMEM),
        scratch_shapes=[pltpu.VMEM((half, ranks), f32)],
        compiler_params=pltpu.CompilerParams(vmem_limit_bytes=24 << 20),
        cost_estimate=pl.CostEstimate(flops=400_000_000, bytes_accessed=6_000_000, transcendentals=0),
    )(where, hidden, low_grad, low_rank, c_all)

    returned = exchange(back)

    swap = [(f, f ^ 1) for f in range(spread)]
    pair = own.astype(f32) + lax.ppermute(other, "fsdp", swap).astype(f32)
    halved = pair.astype(bf16)
    total = pair[0]
    for dz in range(1, zs):
        moves = [(f, (f + 2 * dz) % spread) for f in range(spread)]
        total = total + lax.ppermute(halved[dz], "fsdp", moves).astype(f32)
    adapter_second_gradient = total[None, :ranks]
    adapter_first_gradient = jnp.concatenate(
        [
            total[ranks : ranks + 16, :ranks],
            total[ranks : ranks + 16, ranks:],
            total[ranks + 16 :, :ranks],
        ],
        axis=0,
    )[None]

    token_input_gradient, gate_weight_gradient = pl.pallas_call(
        lambda *refs: combine_kernel(*refs, experts=experts),
        out_shape=(
            jax.ShapeDtypeStruct((tok_rows, width), bf16),
            jax.ShapeDtypeStruct((tok_rows, top), bf16),
        ),
        in_specs=[VMEM] * 2,
        out_specs=(VMEM, VMEM),
        compiler_params=pltpu.CompilerParams(vmem_limit_bytes=32 << 20),
    )(routed_expert_index, returned)
    return (
        token_input_gradient,
        gate_weight_gradient,
        adapter_first_gradient,
        adapter_second_gradient,
    )


def solution(mesh):
    in_specs = (
        P(("fsdp", "expert"), None),
        P(("fsdp", "expert"), None),
        P(("fsdp", "expert"), None),
        P(("fsdp", "expert"), None),
        P(("fsdp", "expert")),
        P("expert", "fsdp", None),
        P("expert", "fsdp", None),
        P("expert", None, "fsdp"),
        P("expert", "fsdp", None),
        P("expert", None, "fsdp"),
    )
    out_specs = (
        P(("fsdp", "expert"), None),
        P(("fsdp", "expert"), None),
        P("expert", "fsdp", None),
        P("expert", None, "fsdp"),
    )
    return jax.shard_map(shards, mesh=mesh, in_specs=in_specs, out_specs=out_specs, check_vma=False)
```

```python
import jax
import jax.numpy as jnp
from jax import lax
from jax.experimental import pallas as pl
from jax.experimental.pallas import tpu as pltpu
from jax.sharding import PartitionSpec as P

RANK = 32
TENANTS = 4
ADAPTER_SCALE = 2.0
CAPACITY = 20
MAIN = 16
SPARE = CAPACITY - MAIN
QUARTERS = MAIN // SPARE
LANES = 128
SPARE_LANE = 8
TILE = 256
CHUNKS = 4
LIMIT = 54
BACK = 1024

bf16 = jnp.bfloat16
f32 = jnp.float32


def contract(left, right, left_dim, right_dim):
    return lax.dot_general(
        left, right, (((left_dim,), (right_dim,)), ((), ())), preferred_element_type=f32
    )


def iota(shape, dim):
    return lax.broadcasted_iota(jnp.int32, shape, dim)


def slot_places(ids, experts):
    rows, top = ids.shape
    lower = (iota((rows, rows), 1) < iota((rows, rows), 0)).astype(f32).astype(bf16)
    named = iota((rows, LANES), 1)
    total = jnp.zeros((1, LANES), f32)
    places = []
    for j in range(top):
        expert = ids[:, j : j + 1]
        onehot = (named == expert).astype(f32)
        before = contract(lower, onehot.astype(bf16), 1, 0) + total
        total = total + jnp.sum(onehot, axis=0, keepdims=True)
        rank = jnp.sum(before * onehot, axis=1, keepdims=True).astype(jnp.int32)
        main = jnp.where(rank < MAIN, expert * MAIN + rank, -1)
        spare = jnp.where(rank < MAIN, -MAIN * experts, expert * MAIN + rank - MAIN)
        places.append((main, spare))
    return places


def placed(place, slots):
    return (iota((place.shape[0], slots), 1) == place).astype(f32).astype(bf16)


def pack_kernel(gate_hbm, up_hbm, down_hbm, second_hbm, out_hbm, down, second, held, sems):
    half = gate_hbm.shape[1]
    cols = out_hbm.shape[1]
    spans = (pl.ds(0, half), pl.ds(half, half), pl.ds(2 * half, cols - 2 * half))
    loads = [
        pltpu.make_async_copy(down_hbm, down, sems.at[0]),
        pltpu.make_async_copy(second_hbm, second, sems.at[1]),
        pltpu.make_async_copy(gate_hbm, held.at[:, spans[0]], sems.at[2]),
        pltpu.make_async_copy(up_hbm, held.at[:, spans[1]], sems.at[3]),
    ]
    stores = [
        pltpu.make_async_copy(held.at[:, span], out_hbm.at[:, span], sems.at[4 + a])
        for a, span in enumerate(spans)
    ]
    for copy in loads:
        copy.start()
    loads[0].wait()
    held[:, 2 * half : 3 * half] = down[...].T
    loads[1].wait()
    held[:, 3 * half :] = second[...].T
    stores[2].start()
    loads[2].wait()
    stores[0].start()
    loads[3].wait()
    stores[1].start()
    for copy in stores:
        copy.wait()


def dispatch_kernel(ids_ref, gate_ref, tenant_ref, tok_ref, cot_ref, x_ref, c_ref, experts):
    width = tok_ref.shape[1]
    part = width // QUARTERS
    slots = experts * MAIN
    places = slot_places(ids_ref[...], experts)
    main = sum(placed(m, slots) for m, _ in places)
    spare = [sum(placed(s + SPARE * q, slots) for _, s in places) for q in range(QUARTERS)]
    for src, dst in ((tok_ref, x_ref), (cot_ref, c_ref)):
        for q in range(QUARTERS):
            cols = slice(q * part, (q + 1) * part)
            dst[:, cols] = contract(main, src[:, cols], 0, 0).astype(bf16)
        last = jnp.zeros((slots, part), f32)
        for q in range(QUARTERS):
            last = last + contract(spare[q], src[:, q * part : (q + 1) * part], 0, 0)
        dst[:, width : width + part] = last.astype(bf16)
    lane = iota((tok_ref.shape[0], LANES), 1)
    tenant = tenant_ref[...]
    meta = jnp.zeros((slots, LANES), f32)
    for j, (m, s) in enumerate(places):
        gate = gate_ref[:, j : j + 1].astype(f32)
        for place, base in ((m, 0), (s, SPARE_LANE)):
            cols = jnp.where(lane == base, gate, (lane - base - 1 == tenant).astype(f32))
            meta = meta + contract(placed(place, slots), cols.astype(bf16), 0, 0)
    c_ref[:, width + part :] = meta.astype(bf16)


def combine_kernel(ids_ref, r_ref, tok_ref, gate_ref, experts):
    width = tok_ref.shape[1]
    part = width // QUARTERS
    slots = experts * MAIN
    places = slot_places(ids_ref[...], experts)
    main = sum(placed(m, slots) for m, _ in places)
    for q in range(QUARTERS):
        spare = sum(placed(s + SPARE * q, slots) for _, s in places)
        cols = slice(q * part, (q + 1) * part)
        both = contract(main, r_ref[:, cols], 1, 0) + contract(
            spare, r_ref[:, width : width + part], 1, 0
        )
        tok_ref[:, cols] = both.astype(bf16)
    meta = r_ref[:, width + part :]
    for j, (m, s) in enumerate(places):
        a = contract(placed(m, slots), meta, 1, 0)[:, 0:1]
        b = contract(placed(s, slots), meta, 1, 0)[:, SPARE_LANE : SPARE_LANE + 1]
        gate_ref[:, j : j + 1] = (a + b).astype(bf16)


def chosen(q, spares, slots):
    row = iota((spares, slots), 0)
    return (
        (iota((spares, slots), 1) == (row >> 2) * MAIN + q * SPARE + (row & 3))
        .astype(f32)
        .astype(bf16)
    )


def unfold_rows(src_ref, dst_ref):
    width = dst_ref.shape[1]
    part = width // QUARTERS
    slots = src_ref.shape[0]
    spares = slots // QUARTERS
    dst_ref[:slots, :] = src_ref[:, :width]
    for q in range(QUARTERS):
        dst_ref[slots:, q * part : (q + 1) * part] = contract(
            chosen(q, spares, slots), src_ref[:, width : width + part], 1, 0
        ).astype(bf16)


def unfold_cot_kernel(src_ref, dst_ref, mask_ref, gate_ref):
    unfold_rows(src_ref, dst_ref)
    slots = src_ref.shape[0]
    spares = slots // QUARTERS
    lanes = mask_ref.shape[1]
    meta = src_ref[:, src_ref.shape[1] - LANES :]
    meta_spare = contract(chosen(0, spares, slots), meta, 1, 0).astype(bf16)
    lane_in, lane_out = iota((LANES, lanes), 0), iota((LANES, lanes), 1)
    for rows, block, base in ((slice(0, slots), meta, 0), (slice(slots, None), meta_spare, SPARE_LANE)):
        tenant = (lane_in - base - 1 == lane_out // RANK).astype(f32).astype(bf16)
        weight = (lane_in == base).astype(f32).astype(bf16)
        mask_ref[rows, :] = contract(block, tenant, 1, 0)
        gate_ref[rows, :] = contract(block, weight, 1, 0)


def expert_kernel(
    x_hbm, c_hbm, w_hbm, a1_hbm, mask_hbm, gate_hbm,
    rg_hbm, hid_hbm, low_grad_hbm, lowt_hbm,
    xs, cs, w, a1_ref, mask_ref, gate_ref,
    rg_ref, hid, low_grad_ref, lowt_ref,
    acc, hga, parts, spare_rows, dots, sems,
):
    rows, width = xs.shape
    half = hid.shape[1]
    part = width // QUARTERS
    slots = rg_ref.shape[0]
    spares = rows - slots
    wide = 2 * half
    depth = width // CHUNKS

    pending = []

    def begin(src, dst):
        copy = pltpu.make_async_copy(src, dst, sems.at[len(pending)])
        copy.start()
        pending.append(copy)
        return copy

    chunks = []
    for q in range(CHUNKS):
        cols = pl.ds(q * depth, depth)
        chunks.append(
            (
                begin(x_hbm.at[:, cols], xs.at[:, cols]),
                begin(w_hbm.at[cols, :], w.at[cols, :]),
                begin(c_hbm.at[:, cols], cs.at[:, cols]),
            )
        )
    small = [begin(a1_hbm, a1_ref), begin(mask_hbm, mask_ref), begin(gate_hbm, gate_ref)]

    for q in range(CHUNKS):
        cols = slice(q * depth, (q + 1) * depth)
        for copy in chunks[q]:
            copy.wait()
        for rows_ref, out in ((xs, slice(0, wide)), (cs, slice(wide, None))):
            got = contract(rows_ref[:, cols], w[cols, out], 1, 0)
            if q == 0:
                acc[:, out] = got
            else:
                acc[:, out] += got
    for copy in small:
        copy.wait()

    step = 320

    @pl.loop(0, rows // step)
    def _(i):
        r = pl.ds(pl.multiple_of(i * step, step), step)
        pre_gate, pre_up = acc[r, :half], acc[r, half:wide]
        hid[r, :] = (pre_gate * jax.nn.sigmoid(pre_gate) * pre_up).astype(bf16)

    mask, gate = mask_ref[...], gate_ref[...]
    a1 = a1_ref[...]
    cot_low = acc[:, wide + half :] * mask
    low_grad = (ADAPTER_SCALE * gate * cot_low).astype(bf16)
    low_grad_ref[...] = low_grad
    hga[...] = contract(low_grad, a1, 1, 1)
    low = (contract(hid[...], a1, 1, 0) * mask).astype(bf16).astype(f32)
    acc[:, wide + half :] = ADAPTER_SCALE * low * cot_low
    lowt_ref[...] = (ADAPTER_SCALE * gate * low).astype(bf16)

    @pl.loop(0, rows // step)
    def _(i):
        r = pl.ds(pl.multiple_of(i * step, step), step)
        pre_gate, pre_up, cot_down = acc[r, :half], acc[r, half:wide], acc[r, wide : wide + half]
        s = jax.nn.sigmoid(pre_gate)
        grad = gate_ref[r, 0:1] * cot_down + hga[r, :]
        parts[r, half:] = (grad * (pre_gate * s)).astype(bf16)
        parts[r, :half] = (grad * pre_up * s * (1.0 + pre_gate * (1.0 - s))).astype(bf16)
        dot = jnp.sum(hid[r, :].astype(f32) * cot_down, axis=1, keepdims=True) + jnp.sum(
            acc[r, wide + half :], axis=1, keepdims=True
        )
        dots[r, :] = jnp.broadcast_to(dot, (step, LANES)).astype(bf16)

    sent = [
        begin(hid, hid_hbm),
        begin(low_grad_ref, low_grad_hbm),
        begin(lowt_ref, lowt_hbm),
    ]
    lane = iota((slots, LANES), 1)
    spare_dots = contract(chosen(0, spares, slots), dots[slots:, :], 0, 0)
    rg_ref[:, width + part :] = jnp.where(
        lane == 0, dots[:slots, :].astype(f32), jnp.where(lane == SPARE_LANE, spare_dots, 0.0)
    ).astype(bf16)
    for d in range(width // BACK):
        cols = slice(d * BACK, (d + 1) * BACK)
        got = contract(parts[...], w[cols, :wide], 1, 1).astype(bf16)
        rg_ref[:, cols] = got[:slots]
        spare_rows[:, cols] = got[slots:]
        place = pl.ds(d * BACK, BACK)
        sent.append(begin(rg_ref.at[:, place], rg_hbm.at[:, place]))

    last = jnp.zeros((slots, part), f32)
    for q in range(QUARTERS):
        last = last + contract(
            chosen(q, spares, slots), spare_rows[:, q * part : (q + 1) * part], 0, 0
        )
    rg_ref[:, width : width + part] = last.astype(bf16)
    place = pl.ds(width, part + LANES)
    sent.append(begin(rg_ref.at[:, place], rg_hbm.at[:, place]))
    for copy in sent:
        copy.wait()


def adapter_kernel(where_ref, hid_ref, low_grad_ref, lowt_ref, c_ref, own_ref, other_ref, first):
    ranks = low_grad_ref.shape[1]
    z, core = where_ref[0], where_ref[1]
    zs = own_ref.shape[0]
    share = first.shape[0] // (2 * zs)
    first[...] = contract(hid_ref[...], low_grad_ref[...], 0, 0)
    lowt = lowt_ref[...].T

    @pl.loop(0, zs)
    def _(dz):
        for ref, side in ((other_ref, 1 - core), (own_ref, core)):
            f = lax.rem(z + dz, zs) * 2 + side
            cols = pl.ds(pl.multiple_of(f * TILE, TILE), TILE)
            ref[dz, :ranks, :] = contract(lowt, c_ref[:, cols], 1, 0).astype(bf16)
            at = pl.multiple_of(f * share, 16)
            block = first[pl.ds(at, share), :].astype(bf16)
            ref[dz, ranks : ranks + 16, :ranks] = block[:16]
            ref[dz, ranks : ranks + 16, ranks:] = block[16:32]
            ref[dz, ranks + 16 :, :ranks] = block[32:48]
            ref[dz, ranks + 16 :, ranks:] = jnp.zeros((16, TILE - ranks), bf16)


VMEM = pl.BlockSpec(memory_space=pltpu.VMEM)
ANY = pl.BlockSpec(memory_space=pl.ANY)
SMEM = pl.BlockSpec(memory_space=pltpu.SMEM)


def shards(
    tokens,
    cotangent,
    routed_expert_index,
    router_gate_weights,
    token_tenant_index,
    frozen_gate_weight,
    frozen_up_weight,
    frozen_down_weight,
    adapter_first_factors,
    adapter_second_factors,
):
    experts, spread = lax.axis_size("expert"), lax.axis_size("fsdp")
    tok_rows, top = routed_expert_index.shape
    width = tokens.shape[1]
    half = frozen_gate_weight.shape[2]
    ranks = adapter_first_factors.shape[2]
    part = width // QUARTERS
    slots = experts * MAIN
    spares = slots // QUARTERS
    rows = slots + spares
    cols = 3 * half + ranks
    shard = frozen_gate_weight.shape[1]
    zs = spread // 2
    here = lax.axis_index("fsdp")
    where = jnp.stack([here // 2, here % 2]).astype(jnp.int32)

    packed = pl.pallas_call(
        pack_kernel,
        name="pack_weights",
        out_shape=jax.ShapeDtypeStruct((shard, cols), bf16),
        in_specs=[ANY] * 4,
        out_specs=ANY,
        scratch_shapes=[
            pltpu.VMEM((half, shard), bf16),
            pltpu.VMEM((ranks, shard), bf16),
            pltpu.VMEM((shard, cols), bf16),
            pltpu.SemaphoreType.DMA((7,)),
        ],
        compiler_params=pltpu.CompilerParams(vmem_limit_bytes=60 << 20),
    )(
        frozen_gate_weight[0],
        frozen_up_weight[0],
        frozen_down_weight[0],
        adapter_second_factors[0],
    )
    weights = lax.all_gather(packed, "fsdp", axis=0, tiled=True)

    x_send, c_send = pl.pallas_call(
        lambda *refs: dispatch_kernel(*refs, experts=experts),
        out_shape=(
            jax.ShapeDtypeStruct((slots, width + part), bf16),
            jax.ShapeDtypeStruct((slots, width + part + LANES), bf16),
        ),
        in_specs=[VMEM] * 5,
        out_specs=(VMEM, VMEM),
        compiler_params=pltpu.CompilerParams(vmem_limit_bytes=40 << 20),
    )(
        routed_expert_index,
        router_gate_weights,
        token_tenant_index.reshape(tok_rows, 1),
        tokens,
        cotangent,
    )

    def exchange(rows_2d):
        block = rows_2d.reshape(experts, MAIN, rows_2d.shape[1])
        return lax.all_to_all(block, "expert", split_axis=0, concat_axis=0, tiled=True).reshape(
            rows_2d.shape
        )

    first_full = lax.all_to_all(
        jnp.broadcast_to(adapter_first_factors, (spread,) + adapter_first_factors.shape[1:]),
        "fsdp",
        split_axis=0,
        concat_axis=0,
        tiled=True,
    ).reshape(half, ranks)
    x_send, c_send, first_full = lax.optimization_barrier((x_send, c_send, first_full))
    x_rows, c_rows = exchange(x_send), exchange(c_send)

    x_all = pl.pallas_call(
        unfold_rows,
        name="unfold_tokens",
        out_shape=jax.ShapeDtypeStruct((rows, width), bf16),
        in_specs=[VMEM],
        out_specs=VMEM,
        compiler_params=pltpu.CompilerParams(vmem_limit_bytes=24 << 20),
    )(x_rows)
    c_all, mask, gate = pl.pallas_call(
        unfold_cot_kernel,
        name="unfold_cotangent",
        out_shape=(
            jax.ShapeDtypeStruct((rows, width), bf16),
            jax.ShapeDtypeStruct((rows, ranks), f32),
            jax.ShapeDtypeStruct((rows, ranks), f32),
        ),
        in_specs=[VMEM],
        out_specs=(VMEM, VMEM, VMEM),
        compiler_params=pltpu.CompilerParams(vmem_limit_bytes=24 << 20),
    )(c_rows)

    back, hidden, low_grad, low_rank = pl.pallas_call(
        expert_kernel,
        name="expert",
        out_shape=(
            jax.ShapeDtypeStruct((slots, width + part + LANES), bf16),
            jax.ShapeDtypeStruct((rows, half), bf16),
            jax.ShapeDtypeStruct((rows, ranks), bf16),
            jax.ShapeDtypeStruct((rows, ranks), bf16),
        ),
        in_specs=[ANY] * 6,
        out_specs=(ANY, ANY, ANY, ANY),
        scratch_shapes=[
            pltpu.VMEM((rows, width), bf16),
            pltpu.VMEM((rows, width), bf16),
            pltpu.VMEM((width, cols), bf16),
            pltpu.VMEM((half, ranks), bf16),
            pltpu.VMEM((rows, ranks), f32),
            pltpu.VMEM((rows, ranks), f32),
            pltpu.VMEM((slots, width + part + LANES), bf16),
            pltpu.VMEM((rows, half), bf16),
            pltpu.VMEM((rows, ranks), bf16),
            pltpu.VMEM((rows, ranks), bf16),
            pltpu.VMEM((rows, cols), f32),
            pltpu.VMEM((rows, half), f32),
            pltpu.VMEM((rows, 2 * half), bf16),
            pltpu.VMEM((spares, width), bf16),
            pltpu.VMEM((rows, LANES), bf16),
            pltpu.SemaphoreType.DMA((3 * CHUNKS + 7 + width // BACK,)),
        ],
        compiler_params=pltpu.CompilerParams(vmem_limit_bytes=LIMIT << 20),
    )(x_all, c_all, weights, first_full, mask, gate)

    own, other = pl.pallas_call(
        adapter_kernel,
        name="adapters",
        out_shape=(
            jax.ShapeDtypeStruct((zs, ranks + 32, TILE), bf16),
            jax.ShapeDtypeStruct((zs, ranks + 32, TILE), bf16),
        ),
        in_specs=[SMEM, VMEM, VMEM, VMEM, VMEM],
        out_specs=(VMEM, VMEM),
        scratch_shapes=[pltpu.VMEM((half, ranks), f32)],
        compiler_params=pltpu.CompilerParams(vmem_limit_bytes=24 << 20),
        cost_estimate=pl.CostEstimate(flops=400_000_000, bytes_accessed=6_000_000, transcendentals=0),
    )(where, hidden, low_grad, low_rank, c_all)

    returned = exchange(back)

    swap = [(f, f ^ 1) for f in range(spread)]
    pair = own.astype(f32) + lax.ppermute(other, "fsdp", swap).astype(f32)
    halved = pair.astype(bf16)
    total = pair[0]
    for dz in range(1, zs):
        moves = [(f, (f + 2 * dz) % spread) for f in range(spread)]
        total = total + lax.ppermute(halved[dz], "fsdp", moves).astype(f32)
    adapter_second_gradient = total[None, :ranks]
    adapter_first_gradient = jnp.concatenate(
        [
            total[ranks : ranks + 16, :ranks],
            total[ranks : ranks + 16, ranks:],
            total[ranks + 16 :, :ranks],
        ],
        axis=0,
    )[None]

    token_input_gradient, gate_weight_gradient = pl.pallas_call(
        lambda *refs: combine_kernel(*refs, experts=experts),
        out_shape=(
            jax.ShapeDtypeStruct((tok_rows, width), bf16),
            jax.ShapeDtypeStruct((tok_rows, top), bf16),
        ),
        in_specs=[VMEM] * 2,
        out_specs=(VMEM, VMEM),
        compiler_params=pltpu.CompilerParams(vmem_limit_bytes=32 << 20),
    )(routed_expert_index, returned)
    return (
        token_input_gradient,
        gate_weight_gradient,
        adapter_first_gradient,
        adapter_second_gradient,
    )


def solution(mesh):
    in_specs = (
        P(("fsdp", "expert"), None),
        P(("fsdp", "expert"), None),
        P(("fsdp", "expert"), None),
        P(("fsdp", "expert"), None),
        P(("fsdp", "expert")),
        P("expert", "fsdp", None),
        P("expert", "fsdp", None),
        P("expert", None, "fsdp"),
        P("expert", "fsdp", None),
        P("expert", None, "fsdp"),
    )
    out_specs = (
        P(("fsdp", "expert"), None),
        P(("fsdp", "expert"), None),
        P("expert", "fsdp", None),
        P("expert", None, "fsdp"),
    )
    return jax.shard_map(shards, mesh=mesh, in_specs=in_specs, out_specs=out_specs, check_vma=False)
```

```python
import jax
import jax.numpy as jnp
from jax import lax
from jax.experimental import pallas as pl
from jax.experimental.pallas import tpu as pltpu
from jax.sharding import PartitionSpec as P

RANK = 32
TENANTS = 4
ADAPTER_SCALE = 2.0
CAPACITY = 20
MAIN = 16
SPARE = CAPACITY - MAIN
QUARTERS = MAIN // SPARE
LANES = 128
SPARE_LANE = 8
TILE = 256
CHUNKS = 4
LIMIT = 54
BACK = 1024

bf16 = jnp.bfloat16
f32 = jnp.float32


def contract(left, right, left_dim, right_dim):
    return lax.dot_general(
        left, right, (((left_dim,), (right_dim,)), ((), ())), preferred_element_type=f32
    )


def iota(shape, dim):
    return lax.broadcasted_iota(jnp.int32, shape, dim)


def slot_places(ids, experts):
    rows, top = ids.shape
    lower = (iota((rows, rows), 1) < iota((rows, rows), 0)).astype(f32).astype(bf16)
    named = iota((rows, LANES), 1)
    total = jnp.zeros((1, LANES), f32)
    places = []
    for j in range(top):
        expert = ids[:, j : j + 1]
        onehot = (named == expert).astype(f32)
        before = contract(lower, onehot.astype(bf16), 1, 0) + total
        total = total + jnp.sum(onehot, axis=0, keepdims=True)
        rank = jnp.sum(before * onehot, axis=1, keepdims=True).astype(jnp.int32)
        main = jnp.where(rank < MAIN, expert * MAIN + rank, -1)
        spare = jnp.where(rank < MAIN, -MAIN * experts, expert * MAIN + rank - MAIN)
        places.append((main, spare))
    return places


def placed(place, slots):
    return (iota((place.shape[0], slots), 1) == place).astype(f32).astype(bf16)


def pack_kernel(gate_hbm, up_hbm, down_hbm, out_hbm, down, held, sems):
    half = gate_hbm.shape[1]
    spans = [pl.ds(a * half, half) for a in range(3)]
    loads = [
        pltpu.make_async_copy(down_hbm, down, sems.at[0]),
        pltpu.make_async_copy(gate_hbm, held.at[:, spans[0]], sems.at[1]),
        pltpu.make_async_copy(up_hbm, held.at[:, spans[1]], sems.at[2]),
    ]
    stores = [
        pltpu.make_async_copy(held.at[:, span], out_hbm.at[:, span], sems.at[3 + a])
        for a, span in enumerate(spans)
    ]
    for copy in loads:
        copy.start()
    loads[0].wait()
    held[:, 2 * half :] = down[...].T
    stores[2].start()
    loads[1].wait()
    stores[0].start()
    loads[2].wait()
    stores[1].start()
    for copy in stores:
        copy.wait()


def dispatch_kernel(ids_ref, gate_ref, tenant_ref, tok_ref, cot_ref, x_ref, c_ref, experts):
    width = tok_ref.shape[1]
    part = width // QUARTERS
    slots = experts * MAIN
    places = slot_places(ids_ref[...], experts)
    main = sum(placed(m, slots) for m, _ in places)
    spare = [sum(placed(s + SPARE * q, slots) for _, s in places) for q in range(QUARTERS)]
    for src, dst in ((tok_ref, x_ref), (cot_ref, c_ref)):
        for q in range(QUARTERS):
            cols = slice(q * part, (q + 1) * part)
            dst[:, cols] = contract(main, src[:, cols], 0, 0).astype(bf16)
        last = jnp.zeros((slots, part), f32)
        for q in range(QUARTERS):
            last = last + contract(spare[q], src[:, q * part : (q + 1) * part], 0, 0)
        dst[:, width : width + part] = last.astype(bf16)
    lane = iota((tok_ref.shape[0], LANES), 1)
    tenant = tenant_ref[...]
    meta = jnp.zeros((slots, LANES), f32)
    for j, (m, s) in enumerate(places):
        gate = gate_ref[:, j : j + 1].astype(f32)
        for place, base in ((m, 0), (s, SPARE_LANE)):
            cols = jnp.where(lane == base, gate, (lane - base - 1 == tenant).astype(f32))
            meta = meta + contract(placed(place, slots), cols.astype(bf16), 0, 0)
    c_ref[:, width + part :] = meta.astype(bf16)


def combine_kernel(ids_ref, r_ref, tok_ref, gate_ref, experts):
    width = tok_ref.shape[1]
    part = width // QUARTERS
    slots = experts * MAIN
    places = slot_places(ids_ref[...], experts)
    main = sum(placed(m, slots) for m, _ in places)
    for q in range(QUARTERS):
        spare = sum(placed(s + SPARE * q, slots) for _, s in places)
        cols = slice(q * part, (q + 1) * part)
        both = contract(main, r_ref[:, cols], 1, 0) + contract(
            spare, r_ref[:, width : width + part], 1, 0
        )
        tok_ref[:, cols] = both.astype(bf16)
    meta = r_ref[:, width + part :]
    for j, (m, s) in enumerate(places):
        a = contract(placed(m, slots), meta, 1, 0)[:, 0:1]
        b = contract(placed(s, slots), meta, 1, 0)[:, SPARE_LANE : SPARE_LANE + 1]
        gate_ref[:, j : j + 1] = (a + b).astype(bf16)


def chosen(q, spares, slots):
    row = iota((spares, slots), 0)
    return (
        (iota((spares, slots), 1) == (row >> 2) * MAIN + q * SPARE + (row & 3))
        .astype(f32)
        .astype(bf16)
    )


def unfold_rows(src_ref, dst_ref):
    width = dst_ref.shape[1]
    part = width // QUARTERS
    slots = src_ref.shape[0]
    spares = slots // QUARTERS
    dst_ref[:slots, :] = src_ref[:, :width]
    for q in range(QUARTERS):
        dst_ref[slots:, q * part : (q + 1) * part] = contract(
            chosen(q, spares, slots), src_ref[:, width : width + part], 1, 0
        ).astype(bf16)


def assemble_kernel(where_ref, own_ref, other_ref, a1_ref, a2_ref):
    z, core = where_ref[0], where_ref[1]
    zs = own_ref.shape[0]
    ranks = a2_ref.shape[0]
    share = a1_ref.shape[0] // (2 * zs)
    for i in range(zs):
        for ref, side in ((own_ref, core), (other_ref, 1 - core)):
            f = lax.rem(z + zs - i, zs) * 2 + side
            a2_ref[:, pl.ds(pl.multiple_of(f * TILE, TILE), TILE)] = ref[i, :ranks, :]
            at = pl.multiple_of(f * share, 16)
            a1_ref[pl.ds(at, 16), :] = ref[i, ranks : ranks + 16, :ranks]
            a1_ref[pl.ds(at + 16, 16), :] = ref[i, ranks : ranks + 16, ranks:]
            a1_ref[pl.ds(at + 32, 16), :] = ref[i, ranks + 16 :, :ranks]


def prepare_kernel(
    src_ref, a1_ref, a2_ref, dst_ref, mask_ref, gate_ref, low_ref, grad_ref, hga_ref
):
    unfold_rows(src_ref, dst_ref)
    slots = src_ref.shape[0]
    spares = slots // QUARTERS
    lanes = mask_ref.shape[1]
    meta = src_ref[:, src_ref.shape[1] - LANES :]
    meta_spare = contract(chosen(0, spares, slots), meta, 1, 0).astype(bf16)
    lane_in, lane_out = iota((LANES, lanes), 0), iota((LANES, lanes), 1)
    for rows, block, base in ((slice(0, slots), meta, 0), (slice(slots, None), meta_spare, SPARE_LANE)):
        tenant = (lane_in - base - 1 == lane_out // RANK).astype(f32).astype(bf16)
        weight = (lane_in == base).astype(f32).astype(bf16)
        mask_ref[rows, :] = contract(block, tenant, 1, 0)
        gate_ref[rows, :] = contract(block, weight, 1, 0)

    low = contract(dst_ref[...], a2_ref[...], 1, 1) * mask_ref[...]
    low_ref[...] = low
    grad = (ADAPTER_SCALE * gate_ref[...] * low).astype(bf16)
    grad_ref[...] = grad
    hga_ref[...] = contract(grad, a1_ref[...], 1, 1)


def expert_kernel(
    x_hbm, c_hbm, w_hbm, a1_hbm, mask_hbm, gate_hbm, low_hbm, hga_hbm,
    rg_hbm, hid_hbm, lowt_hbm,
    xs, cs, w, a1_ref, mask_ref, gate_ref, low_ref, hga,
    rg_ref, hid, lowt_ref,
    acc, parts, spare_rows, dots, sems,
):
    rows, width = xs.shape
    half = hid.shape[1]
    part = width // QUARTERS
    slots = rg_ref.shape[0]
    spares = rows - slots
    wide = 2 * half
    depth = width // CHUNKS

    pending = []

    def begin(src, dst):
        copy = pltpu.make_async_copy(src, dst, sems.at[len(pending)])
        copy.start()
        pending.append(copy)
        return copy

    chunks = []
    for q in range(CHUNKS):
        cols = pl.ds(q * depth, depth)
        chunks.append(
            (
                begin(x_hbm.at[:, cols], xs.at[:, cols]),
                begin(w_hbm.at[cols, :], w.at[cols, :]),
                begin(c_hbm.at[:, cols], cs.at[:, cols]),
            )
        )
    small = [
        begin(src, dst)
        for src, dst in (
            (gate_hbm, gate_ref),
            (hga_hbm, hga),
            (a1_hbm, a1_ref),
            (mask_hbm, mask_ref),
            (low_hbm, low_ref),
        )
    ]

    for q in range(CHUNKS):
        cols = slice(q * depth, (q + 1) * depth)
        for copy in chunks[q]:
            copy.wait()
        for rows_ref, out in ((xs, slice(0, wide)), (cs, slice(wide, None))):
            got = contract(rows_ref[:, cols], w[cols, out], 1, 0)
            if q == 0:
                acc[:, out] = got
            else:
                acc[:, out] += got
    for copy in small:
        copy.wait()

    pre_gate, pre_up, cot_down = acc[:, :half], acc[:, half:wide], acc[:, wide:]
    s = jax.nn.sigmoid(pre_gate)
    silu = pre_gate * s
    grad = gate_ref[:, 0:1] * cot_down + hga[...]
    parts[:, half:] = (grad * silu).astype(bf16)
    parts[:, :half] = (grad * pre_up * s * (1.0 + pre_gate * (1.0 - s))).astype(bf16)
    hidden = (silu * pre_up).astype(bf16)
    hid[...] = hidden
    low = (contract(hid[...], a1_ref[...], 1, 0) * mask_ref[...]).astype(bf16).astype(f32)
    lowt_ref[...] = (ADAPTER_SCALE * gate_ref[...] * low).astype(bf16)
    dot = jnp.sum(hidden.astype(f32) * cot_down, axis=1, keepdims=True) + jnp.sum(
        ADAPTER_SCALE * low * low_ref[...], axis=1, keepdims=True
    )
    dots[...] = jnp.broadcast_to(dot, dots.shape).astype(bf16)

    sent = [begin(hid, hid_hbm), begin(lowt_ref, lowt_hbm)]
    lane = iota((slots, LANES), 1)
    spare_dots = contract(chosen(0, spares, slots), dots[slots:, :], 0, 0)
    rg_ref[:, width + part :] = jnp.where(
        lane == 0, dots[:slots, :].astype(f32), jnp.where(lane == SPARE_LANE, spare_dots, 0.0)
    ).astype(bf16)
    for d in range(width // BACK):
        cols = slice(d * BACK, (d + 1) * BACK)
        got = contract(parts[...], w[cols, :wide], 1, 1).astype(bf16)
        rg_ref[:, cols] = got[:slots]
        spare_rows[:, cols] = got[slots:]
        place = pl.ds(d * BACK, BACK)
        sent.append(begin(rg_ref.at[:, place], rg_hbm.at[:, place]))

    last = jnp.zeros((slots, part), f32)
    for q in range(QUARTERS):
        last = last + contract(
            chosen(q, spares, slots), spare_rows[:, q * part : (q + 1) * part], 0, 0
        )
    rg_ref[:, width : width + part] = last.astype(bf16)
    place = pl.ds(width, part + LANES)
    sent.append(begin(rg_ref.at[:, place], rg_hbm.at[:, place]))
    for copy in sent:
        copy.wait()


def adapter_kernel(where_ref, hid_ref, low_grad_ref, lowt_ref, c_ref, own_ref, other_ref, first):
    ranks = low_grad_ref.shape[1]
    z, core = where_ref[0], where_ref[1]
    zs = own_ref.shape[0]
    share = first.shape[0] // (2 * zs)
    first[...] = contract(hid_ref[...], low_grad_ref[...], 0, 0)
    lowt = lowt_ref[...].T

    @pl.loop(0, zs)
    def _(dz):
        for ref, side in ((other_ref, 1 - core), (own_ref, core)):
            f = lax.rem(z + dz, zs) * 2 + side
            cols = pl.ds(pl.multiple_of(f * TILE, TILE), TILE)
            ref[dz, :ranks, :] = contract(lowt, c_ref[:, cols], 1, 0).astype(bf16)
            at = pl.multiple_of(f * share, 16)
            block = first[pl.ds(at, share), :].astype(bf16)
            ref[dz, ranks : ranks + 16, :ranks] = block[:16]
            ref[dz, ranks : ranks + 16, ranks:] = block[16:32]
            ref[dz, ranks + 16 :, :ranks] = block[32:48]
            ref[dz, ranks + 16 :, ranks:] = jnp.zeros((16, TILE - ranks), bf16)


VMEM = pl.BlockSpec(memory_space=pltpu.VMEM)
ANY = pl.BlockSpec(memory_space=pl.ANY)
SMEM = pl.BlockSpec(memory_space=pltpu.SMEM)


def shards(
    tokens,
    cotangent,
    routed_expert_index,
    router_gate_weights,
    token_tenant_index,
    frozen_gate_weight,
    frozen_up_weight,
    frozen_down_weight,
    adapter_first_factors,
    adapter_second_factors,
):
    experts, spread = lax.axis_size("expert"), lax.axis_size("fsdp")
    tok_rows, top = routed_expert_index.shape
    width = tokens.shape[1]
    half = frozen_gate_weight.shape[2]
    ranks = adapter_first_factors.shape[2]
    part = width // QUARTERS
    slots = experts * MAIN
    spares = slots // QUARTERS
    rows = slots + spares
    cols = 3 * half
    shard = frozen_gate_weight.shape[1]
    zs = spread // 2
    here = lax.axis_index("fsdp")
    where = jnp.stack([here // 2, here % 2]).astype(jnp.int32)

    packed = pl.pallas_call(
        pack_kernel,
        name="pack_weights",
        out_shape=jax.ShapeDtypeStruct((shard, cols), bf16),
        in_specs=[ANY] * 3,
        out_specs=ANY,
        scratch_shapes=[
            pltpu.VMEM((half, shard), bf16),
            pltpu.VMEM((shard, cols), bf16),
            pltpu.SemaphoreType.DMA((6,)),
        ],
        compiler_params=pltpu.CompilerParams(vmem_limit_bytes=60 << 20),
    )(frozen_gate_weight[0], frozen_up_weight[0], frozen_down_weight[0])
    packed, first_part, second_part = lax.optimization_barrier(
        (packed, adapter_first_factors[0], adapter_second_factors[0])
    )
    first_rows = [first_part[a * 16 : (a + 1) * 16] for a in range(3)]
    first_rows.append(jnp.zeros_like(first_rows[0]))
    small = jnp.concatenate(
        [
            second_part,
            jnp.concatenate(first_rows[:2], axis=1),
            jnp.concatenate(first_rows[2:], axis=1),
        ],
        axis=0,
    )
    weights = lax.all_gather(packed, "fsdp", axis=0, tiled=True)

    x_send, c_send = pl.pallas_call(
        lambda *refs: dispatch_kernel(*refs, experts=experts),
        out_shape=(
            jax.ShapeDtypeStruct((slots, width + part), bf16),
            jax.ShapeDtypeStruct((slots, width + part + LANES), bf16),
        ),
        in_specs=[VMEM] * 5,
        out_specs=(VMEM, VMEM),
        compiler_params=pltpu.CompilerParams(vmem_limit_bytes=40 << 20),
    )(
        routed_expert_index,
        router_gate_weights,
        token_tenant_index.reshape(tok_rows, 1),
        tokens,
        cotangent,
    )

    def exchange(rows_2d):
        block = rows_2d.reshape(experts, MAIN, rows_2d.shape[1])
        return lax.all_to_all(block, "expert", split_axis=0, concat_axis=0, tiled=True).reshape(
            rows_2d.shape
        )

    def along(block, step):
        return lax.ppermute(
            block, "fsdp", [(f, (f + 2 * step) % spread) for f in range(spread)]
        )

    swap = [(f, f ^ 1) for f in range(spread)]
    low_side, high_side = [small], [small]
    for _ in range(zs // 2 - 1):
        low_side.append(along(low_side[-1], 1))
    for _ in range(zs - zs // 2 - 1):
        high_side.append(along(high_side[-1], -1))
    x_send, c_send, low_side[3], high_side[3] = lax.optimization_barrier(
        (x_send, c_send, low_side[3], high_side[3])
    )
    low_side.append(along(low_side[-1], 1))
    near = jnp.stack(low_side + high_side[:0:-1])
    far = lax.ppermute(near, "fsdp", swap)
    first_full, second_full = pl.pallas_call(
        assemble_kernel,
        name="assemble_adapters",
        out_shape=(
            jax.ShapeDtypeStruct((half, ranks), bf16),
            jax.ShapeDtypeStruct((ranks, width), bf16),
        ),
        in_specs=[SMEM, VMEM, VMEM],
        out_specs=(VMEM, VMEM),
        compiler_params=pltpu.CompilerParams(vmem_limit_bytes=16 << 20),
    )(where, near, far)
    x_rows, c_rows = exchange(x_send), exchange(c_send)

    x_all = pl.pallas_call(
        unfold_rows,
        name="unfold_tokens",
        out_shape=jax.ShapeDtypeStruct((rows, width), bf16),
        in_specs=[VMEM],
        out_specs=VMEM,
        compiler_params=pltpu.CompilerParams(vmem_limit_bytes=24 << 20),
    )(x_rows)
    c_all, mask, gate, cot_low, low_grad, grad_low = pl.pallas_call(
        prepare_kernel,
        name="prepare_cotangent",
        out_shape=(
            jax.ShapeDtypeStruct((rows, width), bf16),
            jax.ShapeDtypeStruct((rows, ranks), f32),
            jax.ShapeDtypeStruct((rows, ranks), f32),
            jax.ShapeDtypeStruct((rows, ranks), f32),
            jax.ShapeDtypeStruct((rows, ranks), bf16),
            jax.ShapeDtypeStruct((rows, half), f32),
        ),
        in_specs=[VMEM, VMEM, VMEM],
        out_specs=(VMEM,) * 6,
        compiler_params=pltpu.CompilerParams(vmem_limit_bytes=60 << 20),
    )(c_rows, first_full, second_full)

    back, hidden, low_rank = pl.pallas_call(
        expert_kernel,
        name="expert",
        out_shape=(
            jax.ShapeDtypeStruct((slots, width + part + LANES), bf16),
            jax.ShapeDtypeStruct((rows, half), bf16),
            jax.ShapeDtypeStruct((rows, ranks), bf16),
        ),
        in_specs=[ANY] * 8,
        out_specs=(ANY, ANY, ANY),
        scratch_shapes=[
            pltpu.VMEM((rows, width), bf16),
            pltpu.VMEM((rows, width), bf16),
            pltpu.VMEM((width, cols), bf16),
            pltpu.VMEM((half, ranks), bf16),
            pltpu.VMEM((rows, ranks), f32),
            pltpu.VMEM((rows, ranks), f32),
            pltpu.VMEM((rows, ranks), f32),
            pltpu.VMEM((rows, half), f32),
            pltpu.VMEM((slots, width + part + LANES), bf16),
            pltpu.VMEM((rows, half), bf16),
            pltpu.VMEM((rows, ranks), bf16),
            pltpu.VMEM((rows, cols), f32),
            pltpu.VMEM((rows, 2 * half), bf16),
            pltpu.VMEM((spares, width), bf16),
            pltpu.VMEM((rows, LANES), bf16),
            pltpu.SemaphoreType.DMA((3 * CHUNKS + 8 + width // BACK,)),
        ],
        compiler_params=pltpu.CompilerParams(vmem_limit_bytes=LIMIT << 20),
    )(x_all, c_all, weights, first_full, mask, gate, cot_low, grad_low)

    own, other = pl.pallas_call(
        adapter_kernel,
        name="adapters",
        out_shape=(
            jax.ShapeDtypeStruct((zs, ranks + 32, TILE), bf16),
            jax.ShapeDtypeStruct((zs, ranks + 32, TILE), bf16),
        ),
        in_specs=[SMEM, VMEM, VMEM, VMEM, VMEM],
        out_specs=(VMEM, VMEM),
        scratch_shapes=[pltpu.VMEM((half, ranks), f32)],
        compiler_params=pltpu.CompilerParams(vmem_limit_bytes=24 << 20),
        cost_estimate=pl.CostEstimate(flops=400_000_000, bytes_accessed=6_000_000, transcendentals=0),
    )(where, hidden, low_grad, low_rank, c_all)

    returned = exchange(back)

    pair = own.astype(f32) + lax.ppermute(other, "fsdp", swap).astype(f32)
    halved = pair.astype(bf16)
    total = pair[0]
    for dz in range(1, zs):
        moves = [(f, (f + 2 * dz) % spread) for f in range(spread)]
        total = total + lax.ppermute(halved[dz], "fsdp", moves).astype(f32)
    adapter_second_gradient = total[None, :ranks]
    adapter_first_gradient = jnp.concatenate(
        [
            total[ranks : ranks + 16, :ranks],
            total[ranks : ranks + 16, ranks:],
            total[ranks + 16 :, :ranks],
        ],
        axis=0,
    )[None]

    token_input_gradient, gate_weight_gradient = pl.pallas_call(
        lambda *refs: combine_kernel(*refs, experts=experts),
        out_shape=(
            jax.ShapeDtypeStruct((tok_rows, width), bf16),
            jax.ShapeDtypeStruct((tok_rows, top), bf16),
        ),
        in_specs=[VMEM] * 2,
        out_specs=(VMEM, VMEM),
        compiler_params=pltpu.CompilerParams(vmem_limit_bytes=32 << 20),
    )(routed_expert_index, returned)
    return (
        token_input_gradient,
        gate_weight_gradient,
        adapter_first_gradient,
        adapter_second_gradient,
    )


def solution(mesh):
    in_specs = (
        P(("fsdp", "expert"), None),
        P(("fsdp", "expert"), None),
        P(("fsdp", "expert"), None),
        P(("fsdp", "expert"), None),
        P(("fsdp", "expert")),
        P("expert", "fsdp", None),
        P("expert", "fsdp", None),
        P("expert", None, "fsdp"),
        P("expert", "fsdp", None),
        P("expert", None, "fsdp"),
    )
    out_specs = (
        P(("fsdp", "expert"), None),
        P(("fsdp", "expert"), None),
        P("expert", "fsdp", None),
        P("expert", None, "fsdp"),
    )
    return jax.shard_map(shards, mesh=mesh, in_specs=in_specs, out_specs=out_specs, check_vma=False)
```

```python
import jax
import jax.numpy as jnp
from jax import lax
from jax.experimental import pallas as pl
from jax.experimental.pallas import tpu as pltpu
from jax.sharding import PartitionSpec as P

RANK = 32
TENANTS = 4
ADAPTER_SCALE = 2.0
CAPACITY = 20
MAIN = 16
SPARE = CAPACITY - MAIN
QUARTERS = MAIN // SPARE
LANES = 128
SPARE_LANE = 8
TILE = 256
CHUNKS = 4
LIMIT = 54
BACK = 1024

bf16 = jnp.bfloat16
f32 = jnp.float32


def contract(left, right, left_dim, right_dim):
    return lax.dot_general(
        left, right, (((left_dim,), (right_dim,)), ((), ())), preferred_element_type=f32
    )


def iota(shape, dim):
    return lax.broadcasted_iota(jnp.int32, shape, dim)


def slot_places(ids, experts):
    rows, top = ids.shape
    lower = (iota((rows, rows), 1) < iota((rows, rows), 0)).astype(f32).astype(bf16)
    named = iota((rows, LANES), 1)
    total = jnp.zeros((1, LANES), f32)
    places = []
    for j in range(top):
        expert = ids[:, j : j + 1]
        onehot = (named == expert).astype(f32)
        before = contract(lower, onehot.astype(bf16), 1, 0) + total
        total = total + jnp.sum(onehot, axis=0, keepdims=True)
        rank = jnp.sum(before * onehot, axis=1, keepdims=True).astype(jnp.int32)
        main = jnp.where(rank < MAIN, expert * MAIN + rank, -1)
        spare = jnp.where(rank < MAIN, -MAIN * experts, expert * MAIN + rank - MAIN)
        places.append((main, spare))
    return places


def placed(place, slots):
    return (iota((place.shape[0], slots), 1) == place).astype(f32).astype(bf16)


def pack_kernel(gate_hbm, up_hbm, down_hbm, out_hbm, down, held, sems):
    half = gate_hbm.shape[1]
    most = down.shape[0]
    spans = [pl.ds(0, half), pl.ds(half, half), pl.ds(2 * half, most)]
    loads = [
        pltpu.make_async_copy(down_hbm.at[pl.ds(0, most), :], down, sems.at[0]),
        pltpu.make_async_copy(gate_hbm, held.at[:, spans[0]], sems.at[1]),
        pltpu.make_async_copy(up_hbm, held.at[:, spans[1]], sems.at[2]),
    ]
    stores = [
        pltpu.make_async_copy(held.at[:, span], out_hbm.at[:, span], sems.at[3 + a])
        for a, span in enumerate(spans)
    ]
    for copy in loads:
        copy.start()
    loads[0].wait()
    held[:, 2 * half :] = down[...].T
    stores[2].start()
    loads[1].wait()
    stores[0].start()
    loads[2].wait()
    stores[1].start()
    for copy in stores:
        copy.wait()


def dispatch_kernel(ids_ref, gate_ref, tenant_ref, tok_ref, cot_ref, x_ref, c_ref, experts):
    width = tok_ref.shape[1]
    part = width // QUARTERS
    slots = experts * MAIN
    places = slot_places(ids_ref[...], experts)
    main = sum(placed(m, slots) for m, _ in places)
    spare = [sum(placed(s + SPARE * q, slots) for _, s in places) for q in range(QUARTERS)]
    for src, dst in ((tok_ref, x_ref), (cot_ref, c_ref)):
        for q in range(QUARTERS):
            cols = slice(q * part, (q + 1) * part)
            dst[:, cols] = contract(main, src[:, cols], 0, 0).astype(bf16)
        last = jnp.zeros((slots, part), f32)
        for q in range(QUARTERS):
            last = last + contract(spare[q], src[:, q * part : (q + 1) * part], 0, 0)
        dst[:, width : width + part] = last.astype(bf16)
    lane = iota((tok_ref.shape[0], LANES), 1)
    tenant = tenant_ref[...]
    meta = jnp.zeros((slots, LANES), f32)
    for j, (m, s) in enumerate(places):
        gate = gate_ref[:, j : j + 1].astype(f32)
        for place, base in ((m, 0), (s, SPARE_LANE)):
            cols = jnp.where(lane == base, gate, (lane - base - 1 == tenant).astype(f32))
            meta = meta + contract(placed(place, slots), cols.astype(bf16), 0, 0)
    c_ref[:, width + part :] = meta.astype(bf16)


def combine_kernel(ids_ref, r_ref, tok_ref, gate_ref, experts):
    width = tok_ref.shape[1]
    part = width // QUARTERS
    slots = experts * MAIN
    places = slot_places(ids_ref[...], experts)
    main = sum(placed(m, slots) for m, _ in places)
    for q in range(QUARTERS):
        spare = sum(placed(s + SPARE * q, slots) for _, s in places)
        cols = slice(q * part, (q + 1) * part)
        both = contract(main, r_ref[:, cols], 1, 0) + contract(
            spare, r_ref[:, width : width + part], 1, 0
        )
        tok_ref[:, cols] = both.astype(bf16)
    meta = r_ref[:, width + part :]
    for j, (m, s) in enumerate(places):
        a = contract(placed(m, slots), meta, 1, 0)[:, 0:1]
        b = contract(placed(s, slots), meta, 1, 0)[:, SPARE_LANE : SPARE_LANE + 1]
        gate_ref[:, j : j + 1] = (a + b).astype(bf16)


def chosen(q, spares, slots):
    row = iota((spares, slots), 0)
    return (
        (iota((spares, slots), 1) == (row >> 2) * MAIN + q * SPARE + (row & 3))
        .astype(f32)
        .astype(bf16)
    )


def unfold_rows(src_ref, dst_ref):
    width = dst_ref.shape[1]
    part = width // QUARTERS
    slots = src_ref.shape[0]
    spares = slots // QUARTERS
    dst_ref[:slots, :] = src_ref[:, :width]
    for q in range(QUARTERS):
        dst_ref[slots:, q * part : (q + 1) * part] = contract(
            chosen(q, spares, slots), src_ref[:, width : width + part], 1, 0
        ).astype(bf16)


def assemble_kernel(where_ref, own_ref, other_ref, a1_ref, a2_ref):
    z, core = where_ref[0], where_ref[1]
    zs = own_ref.shape[0]
    ranks, tall = a1_ref.shape[1], a2_ref.shape[0]
    share = a1_ref.shape[0] // (2 * zs)
    for i in range(zs):
        for ref, side in ((own_ref, core), (other_ref, 1 - core)):
            f = lax.rem(z + zs - i, zs) * 2 + side
            a2_ref[:, pl.ds(pl.multiple_of(f * TILE, TILE), TILE)] = ref[i, :tall, :]
            at = pl.multiple_of(f * share, 16)
            a1_ref[pl.ds(at, 16), :] = ref[i, tall : tall + 16, :ranks]
            a1_ref[pl.ds(at + 16, 16), :] = ref[i, tall : tall + 16, ranks:]
            a1_ref[pl.ds(at + 32, 16), :] = ref[i, tall + 16 :, :ranks]


def prepare_kernel(
    src_ref, a1_ref, a2_ref, dst_ref, mask_ref, gate_ref, low_ref, grad_ref, hga_ref, tail_ref
):
    unfold_rows(src_ref, dst_ref)
    slots = src_ref.shape[0]
    spares = slots // QUARTERS
    lanes = mask_ref.shape[1]
    meta = src_ref[:, src_ref.shape[1] - LANES :]
    meta_spare = contract(chosen(0, spares, slots), meta, 1, 0).astype(bf16)
    lane_in, lane_out = iota((LANES, lanes), 0), iota((LANES, lanes), 1)
    for rows, block, base in ((slice(0, slots), meta, 0), (slice(slots, None), meta_spare, SPARE_LANE)):
        tenant = (lane_in - base - 1 == lane_out // RANK).astype(f32).astype(bf16)
        weight = (lane_in == base).astype(f32).astype(bf16)
        mask_ref[rows, :] = contract(block, tenant, 1, 0)
        gate_ref[rows, :] = contract(block, weight, 1, 0)

    both = contract(dst_ref[...], a2_ref[...], 1, 1)
    tail_ref[...] = both[:, lanes:]
    low = both[:, :lanes] * mask_ref[...]
    low_ref[...] = low
    grad = (ADAPTER_SCALE * gate_ref[...] * low).astype(bf16)
    grad_ref[...] = grad
    hga_ref[...] = contract(grad, a1_ref[...], 1, 1)


def expert_kernel(
    x_hbm, c_hbm, w_hbm, a1_hbm, mask_hbm, gate_hbm, low_hbm, hga_hbm, tail_hbm,
    rg_hbm, hid_hbm, lowt_hbm,
    xs, cs, w, a1_ref, mask_ref, gate_ref, low_ref, hga,
    rg_ref, hid, lowt_ref,
    acc, parts, spare_rows, dots, sems,
):
    rows, width = xs.shape
    half = hid.shape[1]
    part = width // QUARTERS
    slots = rg_ref.shape[0]
    spares = rows - slots
    wide = 2 * half
    depth = width // CHUNKS
    packed = w.shape[1]

    pending = []

    def begin(src, dst):
        copy = pltpu.make_async_copy(src, dst, sems.at[len(pending)])
        copy.start()
        pending.append(copy)
        return copy

    chunks = []
    for q in range(CHUNKS):
        cols = pl.ds(q * depth, depth)
        chunks.append(
            (
                begin(x_hbm.at[:, cols], xs.at[:, cols]),
                begin(w_hbm.at[cols, :], w.at[cols, :]),
                begin(c_hbm.at[:, cols], cs.at[:, cols]),
            )
        )
    small = [
        begin(src, dst)
        for src, dst in (
            (gate_hbm, gate_ref),
            (hga_hbm, hga),
            (a1_hbm, a1_ref),
            (mask_hbm, mask_ref),
            (low_hbm, low_ref),
            (tail_hbm, acc.at[:, pl.ds(packed, acc.shape[1] - packed)]),
        )
    ]

    for q in range(CHUNKS):
        cols = slice(q * depth, (q + 1) * depth)
        for copy in chunks[q]:
            copy.wait()
        for rows_ref, out in ((xs, slice(0, wide)), (cs, slice(wide, packed))):
            got = contract(rows_ref[:, cols], w[cols, out], 1, 0)
            if q == 0:
                acc[:, out] = got
            else:
                acc[:, out] += got
    for copy in small:
        copy.wait()

    pre_gate, pre_up, cot_down = acc[:, :half], acc[:, half:wide], acc[:, wide:]
    s = jax.nn.sigmoid(pre_gate)
    silu = pre_gate * s
    grad = gate_ref[:, 0:1] * cot_down + hga[...]
    parts[:, half:] = (grad * silu).astype(bf16)
    parts[:, :half] = (grad * pre_up * s * (1.0 + pre_gate * (1.0 - s))).astype(bf16)
    hidden = (silu * pre_up).astype(bf16)
    hid[...] = hidden
    low = (contract(hid[...], a1_ref[...], 1, 0) * mask_ref[...]).astype(bf16).astype(f32)
    lowt_ref[...] = (ADAPTER_SCALE * gate_ref[...] * low).astype(bf16)
    dot = jnp.sum(hidden.astype(f32) * cot_down, axis=1, keepdims=True) + jnp.sum(
        ADAPTER_SCALE * low * low_ref[...], axis=1, keepdims=True
    )
    dots[...] = jnp.broadcast_to(dot, dots.shape).astype(bf16)

    sent = [begin(hid, hid_hbm), begin(lowt_ref, lowt_hbm)]
    lane = iota((slots, LANES), 1)
    spare_dots = contract(chosen(0, spares, slots), dots[slots:, :], 0, 0)
    rg_ref[:, width + part :] = jnp.where(
        lane == 0, dots[:slots, :].astype(f32), jnp.where(lane == SPARE_LANE, spare_dots, 0.0)
    ).astype(bf16)
    for d in range(width // BACK):
        cols = slice(d * BACK, (d + 1) * BACK)
        got = contract(parts[...], w[cols, :wide], 1, 1).astype(bf16)
        rg_ref[:, cols] = got[:slots]
        spare_rows[:, cols] = got[slots:]
        place = pl.ds(d * BACK, BACK)
        sent.append(begin(rg_ref.at[:, place], rg_hbm.at[:, place]))

    last = jnp.zeros((slots, part), f32)
    for q in range(QUARTERS):
        last = last + contract(
            chosen(q, spares, slots), spare_rows[:, q * part : (q + 1) * part], 0, 0
        )
    rg_ref[:, width : width + part] = last.astype(bf16)
    place = pl.ds(width, part + LANES)
    sent.append(begin(rg_ref.at[:, place], rg_hbm.at[:, place]))
    for copy in sent:
        copy.wait()


def adapter_kernel(where_ref, hid_ref, low_grad_ref, lowt_ref, c_ref, own_ref, other_ref, first):
    ranks = low_grad_ref.shape[1]
    z, core = where_ref[0], where_ref[1]
    zs = own_ref.shape[0]
    share = first.shape[0] // (2 * zs)
    first[...] = contract(hid_ref[...], low_grad_ref[...], 0, 0)
    lowt = lowt_ref[...].T

    @pl.loop(0, zs)
    def _(dz):
        for ref, side in ((other_ref, 1 - core), (own_ref, core)):
            f = lax.rem(z + dz, zs) * 2 + side
            cols = pl.ds(pl.multiple_of(f * TILE, TILE), TILE)
            ref[dz, :ranks, :] = contract(lowt, c_ref[:, cols], 1, 0).astype(bf16)
            at = pl.multiple_of(f * share, 16)
            block = first[pl.ds(at, share), :].astype(bf16)
            ref[dz, ranks : ranks + 16, :ranks] = block[:16]
            ref[dz, ranks : ranks + 16, ranks:] = block[16:32]
            ref[dz, ranks + 16 :, :ranks] = block[32:48]
            ref[dz, ranks + 16 :, ranks:] = jnp.zeros((16, TILE - ranks), bf16)


VMEM = pl.BlockSpec(memory_space=pltpu.VMEM)
ANY = pl.BlockSpec(memory_space=pl.ANY)
SMEM = pl.BlockSpec(memory_space=pltpu.SMEM)


def shards(
    tokens,
    cotangent,
    routed_expert_index,
    router_gate_weights,
    token_tenant_index,
    frozen_gate_weight,
    frozen_up_weight,
    frozen_down_weight,
    adapter_first_factors,
    adapter_second_factors,
):
    experts, spread = lax.axis_size("expert"), lax.axis_size("fsdp")
    tok_rows, top = routed_expert_index.shape
    width = tokens.shape[1]
    half = frozen_gate_weight.shape[2]
    ranks = adapter_first_factors.shape[2]
    part = width // QUARTERS
    slots = experts * MAIN
    spares = slots // QUARTERS
    rows = slots + spares
    cols = 3 * half - LANES
    shard = frozen_gate_weight.shape[1]
    zs = spread // 2
    here = lax.axis_index("fsdp")
    where = jnp.stack([here // 2, here % 2]).astype(jnp.int32)

    packed = pl.pallas_call(
        pack_kernel,
        name="pack_weights",
        out_shape=jax.ShapeDtypeStruct((shard, cols), bf16),
        in_specs=[ANY] * 3,
        out_specs=ANY,
        scratch_shapes=[
            pltpu.VMEM((half - LANES, shard), bf16),
            pltpu.VMEM((shard, cols), bf16),
            pltpu.SemaphoreType.DMA((6,)),
        ],
        compiler_params=pltpu.CompilerParams(vmem_limit_bytes=60 << 20),
    )(frozen_gate_weight[0], frozen_up_weight[0], frozen_down_weight[0])
    packed, first_part, second_part, down_part = lax.optimization_barrier(
        (
            packed,
            adapter_first_factors[0],
            adapter_second_factors[0],
            frozen_down_weight[0, half - LANES :],
        )
    )
    first_rows = [first_part[a * 16 : (a + 1) * 16] for a in range(3)]
    first_rows.append(jnp.zeros_like(first_rows[0]))
    small = jnp.concatenate(
        [
            second_part,
            down_part,
            jnp.concatenate(first_rows[:2], axis=1),
            jnp.concatenate(first_rows[2:], axis=1),
        ],
        axis=0,
    )
    weights = lax.all_gather(packed, "fsdp", axis=0, tiled=True)

    x_send, c_send = pl.pallas_call(
        lambda *refs: dispatch_kernel(*refs, experts=experts),
        out_shape=(
            jax.ShapeDtypeStruct((slots, width + part), bf16),
            jax.ShapeDtypeStruct((slots, width + part + LANES), bf16),
        ),
        in_specs=[VMEM] * 5,
        out_specs=(VMEM, VMEM),
        compiler_params=pltpu.CompilerParams(vmem_limit_bytes=40 << 20),
    )(
        routed_expert_index,
        router_gate_weights,
        token_tenant_index.reshape(tok_rows, 1),
        tokens,
        cotangent,
    )

    def exchange(rows_2d):
        block = rows_2d.reshape(experts, MAIN, rows_2d.shape[1])
        return lax.all_to_all(block, "expert", split_axis=0, concat_axis=0, tiled=True).reshape(
            rows_2d.shape
        )

    def along(block, step):
        return lax.ppermute(
            block, "fsdp", [(f, (f + 2 * step) % spread) for f in range(spread)]
        )

    swap = [(f, f ^ 1) for f in range(spread)]
    low_side, high_side = [small], [small]
    for _ in range(zs // 2 - 1):
        low_side.append(along(low_side[-1], 1))
    for _ in range(zs - zs // 2 - 1):
        high_side.append(along(high_side[-1], -1))
    x_send, c_send, low_side[3], high_side[3] = lax.optimization_barrier(
        (x_send, c_send, low_side[3], high_side[3])
    )
    low_side.append(along(low_side[-1], 1))
    near = jnp.stack(low_side + high_side[:0:-1])
    far = lax.ppermute(near, "fsdp", swap)
    first_full, second_full = pl.pallas_call(
        assemble_kernel,
        name="assemble_adapters",
        out_shape=(
            jax.ShapeDtypeStruct((half, ranks), bf16),
            jax.ShapeDtypeStruct((ranks + LANES, width), bf16),
        ),
        in_specs=[SMEM, VMEM, VMEM],
        out_specs=(VMEM, VMEM),
        compiler_params=pltpu.CompilerParams(vmem_limit_bytes=16 << 20),
    )(where, near, far)
    x_rows, c_rows = exchange(x_send), exchange(c_send)

    x_all = pl.pallas_call(
        unfold_rows,
        name="unfold_tokens",
        out_shape=jax.ShapeDtypeStruct((rows, width), bf16),
        in_specs=[VMEM],
        out_specs=VMEM,
        compiler_params=pltpu.CompilerParams(vmem_limit_bytes=24 << 20),
    )(x_rows)
    c_all, mask, gate, cot_low, low_grad, grad_low, cot_tail = pl.pallas_call(
        prepare_kernel,
        name="prepare_cotangent",
        out_shape=(
            jax.ShapeDtypeStruct((rows, width), bf16),
            jax.ShapeDtypeStruct((rows, ranks), f32),
            jax.ShapeDtypeStruct((rows, ranks), f32),
            jax.ShapeDtypeStruct((rows, ranks), f32),
            jax.ShapeDtypeStruct((rows, ranks), bf16),
            jax.ShapeDtypeStruct((rows, half), f32),
            jax.ShapeDtypeStruct((rows, LANES), f32),
        ),
        in_specs=[VMEM, VMEM, VMEM],
        out_specs=(VMEM,) * 7,
        compiler_params=pltpu.CompilerParams(vmem_limit_bytes=60 << 20),
    )(c_rows, first_full, second_full)

    back, hidden, low_rank = pl.pallas_call(
        expert_kernel,
        name="expert",
        out_shape=(
            jax.ShapeDtypeStruct((slots, width + part + LANES), bf16),
            jax.ShapeDtypeStruct((rows, half), bf16),
            jax.ShapeDtypeStruct((rows, ranks), bf16),
        ),
        in_specs=[ANY] * 9,
        out_specs=(ANY, ANY, ANY),
        scratch_shapes=[
            pltpu.VMEM((rows, width), bf16),
            pltpu.VMEM((rows, width), bf16),
            pltpu.VMEM((width, cols), bf16),
            pltpu.VMEM((half, ranks), bf16),
            pltpu.VMEM((rows, ranks), f32),
            pltpu.VMEM((rows, ranks), f32),
            pltpu.VMEM((rows, ranks), f32),
            pltpu.VMEM((rows, half), f32),
            pltpu.VMEM((slots, width + part + LANES), bf16),
            pltpu.VMEM((rows, half), bf16),
            pltpu.VMEM((rows, ranks), bf16),
            pltpu.VMEM((rows, 3 * half), f32),
            pltpu.VMEM((rows, 2 * half), bf16),
            pltpu.VMEM((spares, width), bf16),
            pltpu.VMEM((rows, LANES), bf16),
            pltpu.SemaphoreType.DMA((3 * CHUNKS + 9 + width // BACK,)),
        ],
        compiler_params=pltpu.CompilerParams(vmem_limit_bytes=LIMIT << 20),
    )(x_all, c_all, weights, first_full, mask, gate, cot_low, grad_low, cot_tail)

    own, other = pl.pallas_call(
        adapter_kernel,
        name="adapters",
        out_shape=(
            jax.ShapeDtypeStruct((zs, ranks + 32, TILE), bf16),
            jax.ShapeDtypeStruct((zs, ranks + 32, TILE), bf16),
        ),
        in_specs=[SMEM, VMEM, VMEM, VMEM, VMEM],
        out_specs=(VMEM, VMEM),
        scratch_shapes=[pltpu.VMEM((half, ranks), f32)],
        compiler_params=pltpu.CompilerParams(vmem_limit_bytes=24 << 20),
        cost_estimate=pl.CostEstimate(flops=400_000_000, bytes_accessed=6_000_000, transcendentals=0),
    )(where, hidden, low_grad, low_rank, c_all)

    returned = exchange(back)

    pair = own.astype(f32) + lax.ppermute(other, "fsdp", swap).astype(f32)
    halved = pair.astype(bf16)
    total = pair[0]
    for dz in range(1, zs):
        moves = [(f, (f + 2 * dz) % spread) for f in range(spread)]
        total = total + lax.ppermute(halved[dz], "fsdp", moves).astype(f32)
    adapter_second_gradient = total[None, :ranks]
    adapter_first_gradient = jnp.concatenate(
        [
            total[ranks : ranks + 16, :ranks],
            total[ranks : ranks + 16, ranks:],
            total[ranks + 16 :, :ranks],
        ],
        axis=0,
    )[None]

    token_input_gradient, gate_weight_gradient = pl.pallas_call(
        lambda *refs: combine_kernel(*refs, experts=experts),
        out_shape=(
            jax.ShapeDtypeStruct((tok_rows, width), bf16),
            jax.ShapeDtypeStruct((tok_rows, top), bf16),
        ),
        in_specs=[VMEM] * 2,
        out_specs=(VMEM, VMEM),
        compiler_params=pltpu.CompilerParams(vmem_limit_bytes=32 << 20),
    )(routed_expert_index, returned)
    return (
        token_input_gradient,
        gate_weight_gradient,
        adapter_first_gradient,
        adapter_second_gradient,
    )


def solution(mesh):
    in_specs = (
        P(("fsdp", "expert"), None),
        P(("fsdp", "expert"), None),
        P(("fsdp", "expert"), None),
        P(("fsdp", "expert"), None),
        P(("fsdp", "expert")),
        P("expert", "fsdp", None),
        P("expert", "fsdp", None),
        P("expert", None, "fsdp"),
        P("expert", "fsdp", None),
        P("expert", None, "fsdp"),
    )
    out_specs = (
        P(("fsdp", "expert"), None),
        P(("fsdp", "expert"), None),
        P("expert", "fsdp", None),
        P("expert", None, "fsdp"),
    )
    return jax.shard_map(shards, mesh=mesh, in_specs=in_specs, out_specs=out_specs, check_vma=False)
```

```python
import jax
import jax.numpy as jnp
from jax import lax
from jax.experimental import pallas as pl
from jax.experimental.pallas import tpu as pltpu
from jax.sharding import PartitionSpec as P

RANK = 32
TENANTS = 4
ADAPTER_SCALE = 2.0
CAPACITY = 20
MAIN = 16
SPARE = CAPACITY - MAIN
QUARTERS = MAIN // SPARE
LANES = 128
SPARE_LANE = 8
TILE = 256
CHUNKS = 4
LIMIT = 54
BACK = 1024

bf16 = jnp.bfloat16
f32 = jnp.float32


def contract(left, right, left_dim, right_dim):
    return lax.dot_general(
        left, right, (((left_dim,), (right_dim,)), ((), ())), preferred_element_type=f32
    )


def iota(shape, dim):
    return lax.broadcasted_iota(jnp.int32, shape, dim)


def slot_places(ids, experts):
    rows, top = ids.shape
    lower = (iota((rows, rows), 1) < iota((rows, rows), 0)).astype(f32).astype(bf16)
    named = iota((rows, LANES), 1)
    total = jnp.zeros((1, LANES), f32)
    places = []
    for j in range(top):
        expert = ids[:, j : j + 1]
        onehot = (named == expert).astype(f32)
        before = contract(lower, onehot.astype(bf16), 1, 0) + total
        total = total + jnp.sum(onehot, axis=0, keepdims=True)
        rank = jnp.sum(before * onehot, axis=1, keepdims=True).astype(jnp.int32)
        main = jnp.where(rank < MAIN, expert * MAIN + rank, -1)
        spare = jnp.where(rank < MAIN, -MAIN * experts, expert * MAIN + rank - MAIN)
        places.append((main, spare))
    return places


def placed(place, slots):
    return (iota((place.shape[0], slots), 1) == place).astype(f32).astype(bf16)


def pack_kernel(gate_hbm, up_hbm, down_hbm, out_hbm, down, held, sems):
    half = gate_hbm.shape[1]
    most = down.shape[0]
    spans = [pl.ds(0, half), pl.ds(half, half), pl.ds(2 * half, most)]
    loads = [
        pltpu.make_async_copy(down_hbm.at[pl.ds(0, most), :], down, sems.at[0]),
        pltpu.make_async_copy(gate_hbm, held.at[:, spans[0]], sems.at[1]),
        pltpu.make_async_copy(up_hbm, held.at[:, spans[1]], sems.at[2]),
    ]
    stores = [
        pltpu.make_async_copy(held.at[:, span], out_hbm.at[:, span], sems.at[3 + a])
        for a, span in enumerate(spans)
    ]
    for copy in loads:
        copy.start()
    loads[0].wait()
    held[:, 2 * half :] = down[...].T
    stores[2].start()
    loads[1].wait()
    stores[0].start()
    loads[2].wait()
    stores[1].start()
    for copy in stores:
        copy.wait()


def dispatch_kernel(ids_ref, gate_ref, tenant_ref, tok_ref, cot_ref, x_ref, c_ref, experts):
    width = tok_ref.shape[1]
    part = width // QUARTERS
    slots = experts * MAIN
    places = slot_places(ids_ref[...], experts)
    main = sum(placed(m, slots) for m, _ in places)
    spare = [sum(placed(s + SPARE * q, slots) for _, s in places) for q in range(QUARTERS)]
    for src, dst in ((tok_ref, x_ref), (cot_ref, c_ref)):
        for q in range(QUARTERS):
            cols = slice(q * part, (q + 1) * part)
            dst[:, cols] = contract(main, src[:, cols], 0, 0).astype(bf16)
        last = jnp.zeros((slots, part), f32)
        for q in range(QUARTERS):
            last = last + contract(spare[q], src[:, q * part : (q + 1) * part], 0, 0)
        dst[:, width : width + part] = last.astype(bf16)
    lane = iota((tok_ref.shape[0], LANES), 1)
    tenant = tenant_ref[...]
    meta = jnp.zeros((slots, LANES), f32)
    for j, (m, s) in enumerate(places):
        gate = gate_ref[:, j : j + 1].astype(f32)
        for place, base in ((m, 0), (s, SPARE_LANE)):
            cols = jnp.where(lane == base, gate, (lane - base - 1 == tenant).astype(f32))
            meta = meta + contract(placed(place, slots), cols.astype(bf16), 0, 0)
    c_ref[:, width + part :] = meta.astype(bf16)


def combine_kernel(ids_ref, r_ref, tok_ref, gate_ref, experts):
    width = tok_ref.shape[1]
    part = width // QUARTERS
    slots = experts * MAIN
    places = slot_places(ids_ref[...], experts)
    main = sum(placed(m, slots) for m, _ in places)
    for q in range(QUARTERS):
        spare = sum(placed(s + SPARE * q, slots) for _, s in places)
        cols = slice(q * part, (q + 1) * part)
        both = contract(main, r_ref[:, cols], 1, 0) + contract(
            spare, r_ref[:, width : width + part], 1, 0
        )
        tok_ref[:, cols] = both.astype(bf16)
    meta = r_ref[:, width + part :]
    for j, (m, s) in enumerate(places):
        a = contract(placed(m, slots), meta, 1, 0)[:, 0:1]
        b = contract(placed(s, slots), meta, 1, 0)[:, SPARE_LANE : SPARE_LANE + 1]
        gate_ref[:, j : j + 1] = (a + b).astype(bf16)


def chosen(q, spares, slots):
    row = iota((spares, slots), 0)
    return (
        (iota((spares, slots), 1) == (row >> 2) * MAIN + q * SPARE + (row & 3))
        .astype(f32)
        .astype(bf16)
    )


def unfold_rows(src_ref, dst_ref):
    width = dst_ref.shape[1]
    part = width // QUARTERS
    slots = src_ref.shape[0]
    spares = slots // QUARTERS
    dst_ref[:slots, :] = src_ref[:, :width]
    for q in range(QUARTERS):
        dst_ref[slots:, q * part : (q + 1) * part] = contract(
            chosen(q, spares, slots), src_ref[:, width : width + part], 1, 0
        ).astype(bf16)


def assemble_kernel(where_ref, own_ref, other_ref, a1_ref, a2_ref):
    z, core = where_ref[0], where_ref[1]
    zs = own_ref.shape[0]
    ranks, tall = a1_ref.shape[1], a2_ref.shape[0]
    share = a1_ref.shape[0] // (2 * zs)
    for i in range(zs):
        for ref, side in ((own_ref, core), (other_ref, 1 - core)):
            f = lax.rem(z + zs - i, zs) * 2 + side
            a2_ref[:, pl.ds(pl.multiple_of(f * TILE, TILE), TILE)] = ref[i, :tall, :]
            at = pl.multiple_of(f * share, 16)
            a1_ref[pl.ds(at, 16), :] = ref[i, tall : tall + 16, :ranks]
            a1_ref[pl.ds(at + 16, 16), :] = ref[i, tall : tall + 16, ranks:]
            a1_ref[pl.ds(at + 32, 16), :] = ref[i, tall + 16 :, :ranks]


def prepare_kernel(
    src_ref, a1_ref, a2_ref, dst_ref, mask_ref, gate_ref, low_ref, grad_ref, hga_ref, tail_ref
):
    unfold_rows(src_ref, dst_ref)
    slots = src_ref.shape[0]
    spares = slots // QUARTERS
    lanes = mask_ref.shape[1]
    meta = src_ref[:, src_ref.shape[1] - LANES :]
    meta_spare = contract(chosen(0, spares, slots), meta, 1, 0).astype(bf16)
    lane_in, lane_out = iota((LANES, lanes), 0), iota((LANES, lanes), 1)
    for rows, block, base in ((slice(0, slots), meta, 0), (slice(slots, None), meta_spare, SPARE_LANE)):
        tenant = (lane_in - base - 1 == lane_out // RANK).astype(f32).astype(bf16)
        weight = (lane_in == base).astype(f32).astype(bf16)
        mask_ref[rows, :] = contract(block, tenant, 1, 0)
        gate_ref[rows, :] = contract(block, weight, 1, 0)

    both = contract(dst_ref[...], a2_ref[...], 1, 1)
    tail_ref[...] = both[:, lanes:]
    low = both[:, :lanes] * mask_ref[...]
    low_ref[...] = low
    grad = (ADAPTER_SCALE * gate_ref[...] * low).astype(bf16)
    grad_ref[...] = grad
    hga_ref[...] = contract(grad, a1_ref[...], 1, 1)


def expert_kernel(
    x_hbm, c_hbm, w_hbm, a1_hbm, mask_hbm, gate_hbm, low_hbm, hga_hbm, tail_hbm,
    rg_hbm, hid_hbm, lowt_hbm,
    xs, cs, w, a1_ref, mask_ref, gate_ref, low_ref, hga,
    rg_ref, hid, lowt_ref,
    acc, parts, spare_rows, dots, sems,
):
    rows, width = xs.shape
    half = hid.shape[1]
    part = width // QUARTERS
    slots = rg_ref.shape[0]
    spares = rows - slots
    wide = 2 * half
    depth = width // CHUNKS
    packed = w.shape[1]

    pending = []

    def begin(src, dst):
        copy = pltpu.make_async_copy(src, dst, sems.at[len(pending)])
        copy.start()
        pending.append(copy)
        return copy

    chunks = []
    for q in range(CHUNKS):
        cols = pl.ds(q * depth, depth)
        chunks.append(
            (
                begin(x_hbm.at[:, cols], xs.at[:, cols]),
                begin(w_hbm.at[cols, :], w.at[cols, :]),
                begin(c_hbm.at[:, cols], cs.at[:, cols]),
            )
        )
    small = [
        begin(src, dst)
        for src, dst in (
            (gate_hbm, gate_ref),
            (hga_hbm, hga),
            (a1_hbm, a1_ref),
            (mask_hbm, mask_ref),
            (low_hbm, low_ref),
            (tail_hbm, acc.at[:, pl.ds(packed, acc.shape[1] - packed)]),
        )
    ]

    for q in range(CHUNKS):
        cols = slice(q * depth, (q + 1) * depth)
        for copy in chunks[q]:
            copy.wait()
        for rows_ref, out in ((xs, slice(0, wide)), (cs, slice(wide, packed))):
            got = contract(rows_ref[:, cols], w[cols, out], 1, 0)
            if q == 0:
                acc[:, out] = got
            else:
                acc[:, out] += got
    for copy in small:
        copy.wait()

    pre_gate, pre_up, cot_down = acc[:, :half], acc[:, half:wide], acc[:, wide:]
    s = jax.nn.sigmoid(pre_gate)
    silu = pre_gate * s
    grad = gate_ref[:, 0:1] * cot_down + hga[...]
    parts[:, half:] = (grad * silu).astype(bf16)
    parts[:, :half] = (grad * pre_up * s * (1.0 + pre_gate * (1.0 - s))).astype(bf16)
    hidden = (silu * pre_up).astype(bf16)
    hid[...] = hidden
    low = (contract(hid[...], a1_ref[...], 1, 0) * mask_ref[...]).astype(bf16).astype(f32)
    lowt_ref[...] = (ADAPTER_SCALE * gate_ref[...] * low).astype(bf16)
    dot = jnp.sum(hidden.astype(f32) * cot_down, axis=1, keepdims=True) + jnp.sum(
        ADAPTER_SCALE * low * low_ref[...], axis=1, keepdims=True
    )
    dots[...] = jnp.broadcast_to(dot, dots.shape).astype(bf16)

    sent = [begin(hid, hid_hbm), begin(lowt_ref, lowt_hbm)]
    lane = iota((slots, LANES), 1)
    spare_dots = contract(chosen(0, spares, slots), dots[slots:, :], 0, 0)
    rg_ref[:, width + part :] = jnp.where(
        lane == 0, dots[:slots, :].astype(f32), jnp.where(lane == SPARE_LANE, spare_dots, 0.0)
    ).astype(bf16)
    for d in range(width // BACK):
        cols = slice(d * BACK, (d + 1) * BACK)
        got = contract(parts[...], w[cols, :wide], 1, 1).astype(bf16)
        rg_ref[:, cols] = got[:slots]
        spare_rows[:, cols] = got[slots:]
        place = pl.ds(d * BACK, BACK)
        sent.append(begin(rg_ref.at[:, place], rg_hbm.at[:, place]))

    last = jnp.zeros((slots, part), f32)
    for q in range(QUARTERS):
        last = last + contract(
            chosen(q, spares, slots), spare_rows[:, q * part : (q + 1) * part], 0, 0
        )
    rg_ref[:, width : width + part] = last.astype(bf16)
    place = pl.ds(width, part + LANES)
    sent.append(begin(rg_ref.at[:, place], rg_hbm.at[:, place]))
    for copy in sent:
        copy.wait()


def adapter_kernel(where_ref, hid_ref, low_grad_ref, lowt_ref, c_ref, own_ref, other_ref, first):
    ranks = low_grad_ref.shape[1]
    z, core = where_ref[0], where_ref[1]
    zs = own_ref.shape[0]
    share = first.shape[0] // (2 * zs)
    first[...] = contract(hid_ref[...], low_grad_ref[...], 0, 0)
    lowt = lowt_ref[...].T

    @pl.loop(0, zs)
    def _(dz):
        for ref, side in ((other_ref, 1 - core), (own_ref, core)):
            f = lax.rem(z + dz, zs) * 2 + side
            cols = pl.ds(pl.multiple_of(f * TILE, TILE), TILE)
            ref[dz, :ranks, :] = contract(lowt, c_ref[:, cols], 1, 0).astype(bf16)
            at = pl.multiple_of(f * share, 16)
            block = first[pl.ds(at, share), :].astype(bf16)
            ref[dz, ranks : ranks + 16, :ranks] = block[:16]
            ref[dz, ranks : ranks + 16, ranks:] = block[16:32]
            ref[dz, ranks + 16 :, :ranks] = block[32:48]
            ref[dz, ranks + 16 :, ranks:] = jnp.zeros((16, TILE - ranks), bf16)


VMEM = pl.BlockSpec(memory_space=pltpu.VMEM)
ANY = pl.BlockSpec(memory_space=pl.ANY)
SMEM = pl.BlockSpec(memory_space=pltpu.SMEM)


def shards(
    tokens,
    cotangent,
    routed_expert_index,
    router_gate_weights,
    token_tenant_index,
    frozen_gate_weight,
    frozen_up_weight,
    frozen_down_weight,
    adapter_first_factors,
    adapter_second_factors,
):
    experts, spread = lax.axis_size("expert"), lax.axis_size("fsdp")
    tok_rows, top = routed_expert_index.shape
    width = tokens.shape[1]
    half = frozen_gate_weight.shape[2]
    ranks = adapter_first_factors.shape[2]
    part = width // QUARTERS
    slots = experts * MAIN
    spares = slots // QUARTERS
    rows = slots + spares
    cols = 3 * half - LANES
    shard = frozen_gate_weight.shape[1]
    zs = spread // 2
    here = lax.axis_index("fsdp")
    where = jnp.stack([here // 2, here % 2]).astype(jnp.int32)

    packed = pl.pallas_call(
        pack_kernel,
        name="pack_weights",
        out_shape=jax.ShapeDtypeStruct((shard, cols), bf16),
        in_specs=[ANY] * 3,
        out_specs=ANY,
        scratch_shapes=[
            pltpu.VMEM((half - LANES, shard), bf16),
            pltpu.VMEM((shard, cols), bf16),
            pltpu.SemaphoreType.DMA((6,)),
        ],
        compiler_params=pltpu.CompilerParams(vmem_limit_bytes=60 << 20),
    )(frozen_gate_weight[0], frozen_up_weight[0], frozen_down_weight[0])
    packed, first_part, second_part, down_part = lax.optimization_barrier(
        (
            packed,
            adapter_first_factors[0],
            adapter_second_factors[0],
            frozen_down_weight[0],
        )
    )
    first_rows = [first_part[a * 16 : (a + 1) * 16] for a in range(3)]
    first_rows.append(jnp.zeros_like(first_rows[0]))
    small = jnp.concatenate(
        [
            second_part,
            down_part[half - LANES :],
            jnp.concatenate(first_rows[:2], axis=1),
            jnp.concatenate(first_rows[2:], axis=1),
        ],
        axis=0,
    )
    weights = lax.all_gather(packed, "fsdp", axis=0, tiled=True)

    x_send, c_send = pl.pallas_call(
        lambda *refs: dispatch_kernel(*refs, experts=experts),
        out_shape=(
            jax.ShapeDtypeStruct((slots, width + part), bf16),
            jax.ShapeDtypeStruct((slots, width + part + LANES), bf16),
        ),
        in_specs=[VMEM] * 5,
        out_specs=(VMEM, VMEM),
        compiler_params=pltpu.CompilerParams(vmem_limit_bytes=40 << 20),
    )(
        routed_expert_index,
        router_gate_weights,
        token_tenant_index.reshape(tok_rows, 1),
        tokens,
        cotangent,
    )

    def exchange(rows_2d):
        block = rows_2d.reshape(experts, MAIN, rows_2d.shape[1])
        return lax.all_to_all(block, "expert", split_axis=0, concat_axis=0, tiled=True).reshape(
            rows_2d.shape
        )

    def along(block, step):
        return lax.ppermute(
            block, "fsdp", [(f, (f + 2 * step) % spread) for f in range(spread)]
        )

    swap = [(f, f ^ 1) for f in range(spread)]
    low_side, high_side = [small], [small]
    for _ in range(2):
        low_side.append(along(low_side[-1], 1))
        high_side.append(along(high_side[-1], -1))
    x_send, c_send, low_side[2], high_side[2] = lax.optimization_barrier(
        (x_send, c_send, low_side[2], high_side[2])
    )
    for _ in range(zs // 2 - 2):
        low_side.append(along(low_side[-1], 1))
    for _ in range(zs - zs // 2 - 3):
        high_side.append(along(high_side[-1], -1))
    near = jnp.stack(low_side + high_side[:0:-1])
    far = lax.ppermute(near, "fsdp", swap)
    first_full, second_full = pl.pallas_call(
        assemble_kernel,
        name="assemble_adapters",
        out_shape=(
            jax.ShapeDtypeStruct((half, ranks), bf16),
            jax.ShapeDtypeStruct((ranks + LANES, width), bf16),
        ),
        in_specs=[SMEM, VMEM, VMEM],
        out_specs=(VMEM, VMEM),
        compiler_params=pltpu.CompilerParams(vmem_limit_bytes=16 << 20),
    )(where, near, far)
    x_rows, c_rows = exchange(x_send), exchange(c_send)

    x_all = pl.pallas_call(
        unfold_rows,
        name="unfold_tokens",
        out_shape=jax.ShapeDtypeStruct((rows, width), bf16),
        in_specs=[VMEM],
        out_specs=VMEM,
        compiler_params=pltpu.CompilerParams(vmem_limit_bytes=24 << 20),
    )(x_rows)
    c_all, mask, gate, cot_low, low_grad, grad_low, cot_tail = pl.pallas_call(
        prepare_kernel,
        name="prepare_cotangent",
        out_shape=(
            jax.ShapeDtypeStruct((rows, width), bf16),
            jax.ShapeDtypeStruct((rows, ranks), f32),
            jax.ShapeDtypeStruct((rows, ranks), f32),
            jax.ShapeDtypeStruct((rows, ranks), f32),
            jax.ShapeDtypeStruct((rows, ranks), bf16),
            jax.ShapeDtypeStruct((rows, half), f32),
            jax.ShapeDtypeStruct((rows, LANES), f32),
        ),
        in_specs=[VMEM, VMEM, VMEM],
        out_specs=(VMEM,) * 7,
        compiler_params=pltpu.CompilerParams(vmem_limit_bytes=60 << 20),
    )(c_rows, first_full, second_full)

    back, hidden, low_rank = pl.pallas_call(
        expert_kernel,
        name="expert",
        out_shape=(
            jax.ShapeDtypeStruct((slots, width + part + LANES), bf16),
            jax.ShapeDtypeStruct((rows, half), bf16),
            jax.ShapeDtypeStruct((rows, ranks), bf16),
        ),
        in_specs=[ANY] * 9,
        out_specs=(ANY, ANY, ANY),
        scratch_shapes=[
            pltpu.VMEM((rows, width), bf16),
            pltpu.VMEM((rows, width), bf16),
            pltpu.VMEM((width, cols), bf16),
            pltpu.VMEM((half, ranks), bf16),
            pltpu.VMEM((rows, ranks), f32),
            pltpu.VMEM((rows, ranks), f32),
            pltpu.VMEM((rows, ranks), f32),
            pltpu.VMEM((rows, half), f32),
            pltpu.VMEM((slots, width + part + LANES), bf16),
            pltpu.VMEM((rows, half), bf16),
            pltpu.VMEM((rows, ranks), bf16),
            pltpu.VMEM((rows, 3 * half), f32),
            pltpu.VMEM((rows, 2 * half), bf16),
            pltpu.VMEM((spares, width), bf16),
            pltpu.VMEM((rows, LANES), bf16),
            pltpu.SemaphoreType.DMA((3 * CHUNKS + 9 + width // BACK,)),
        ],
        compiler_params=pltpu.CompilerParams(vmem_limit_bytes=LIMIT << 20),
    )(x_all, c_all, weights, first_full, mask, gate, cot_low, grad_low, cot_tail)

    own, other = pl.pallas_call(
        adapter_kernel,
        name="adapters",
        out_shape=(
            jax.ShapeDtypeStruct((zs, ranks + 32, TILE), bf16),
            jax.ShapeDtypeStruct((zs, ranks + 32, TILE), bf16),
        ),
        in_specs=[SMEM, VMEM, VMEM, VMEM, VMEM],
        out_specs=(VMEM, VMEM),
        scratch_shapes=[pltpu.VMEM((half, ranks), f32)],
        compiler_params=pltpu.CompilerParams(vmem_limit_bytes=24 << 20),
        cost_estimate=pl.CostEstimate(flops=400_000_000, bytes_accessed=6_000_000, transcendentals=0),
    )(where, hidden, low_grad, low_rank, c_all)

    returned = exchange(back)

    pair = own.astype(f32) + lax.ppermute(other, "fsdp", swap).astype(f32)
    halved = pair.astype(bf16)
    total = pair[0]
    for dz in range(1, zs):
        moves = [(f, (f + 2 * dz) % spread) for f in range(spread)]
        total = total + lax.ppermute(halved[dz], "fsdp", moves).astype(f32)
    adapter_second_gradient = total[None, :ranks]
    adapter_first_gradient = jnp.concatenate(
        [
            total[ranks : ranks + 16, :ranks],
            total[ranks : ranks + 16, ranks:],
            total[ranks + 16 :, :ranks],
        ],
        axis=0,
    )[None]

    token_input_gradient, gate_weight_gradient = pl.pallas_call(
        lambda *refs: combine_kernel(*refs, experts=experts),
        out_shape=(
            jax.ShapeDtypeStruct((tok_rows, width), bf16),
            jax.ShapeDtypeStruct((tok_rows, top), bf16),
        ),
        in_specs=[VMEM] * 2,
        out_specs=(VMEM, VMEM),
        compiler_params=pltpu.CompilerParams(vmem_limit_bytes=32 << 20),
    )(routed_expert_index, returned)
    return (
        token_input_gradient,
        gate_weight_gradient,
        adapter_first_gradient,
        adapter_second_gradient,
    )


def solution(mesh):
    in_specs = (
        P(("fsdp", "expert"), None),
        P(("fsdp", "expert"), None),
        P(("fsdp", "expert"), None),
        P(("fsdp", "expert"), None),
        P(("fsdp", "expert")),
        P("expert", "fsdp", None),
        P("expert", "fsdp", None),
        P("expert", None, "fsdp"),
        P("expert", "fsdp", None),
        P("expert", None, "fsdp"),
    )
    out_specs = (
        P(("fsdp", "expert"), None),
        P(("fsdp", "expert"), None),
        P("expert", "fsdp", None),
        P("expert", None, "fsdp"),
    )
    return jax.shard_map(shards, mesh=mesh, in_specs=in_specs, out_specs=out_specs, check_vma=False)
```
